32 devices in a mesh: blk: 2 (over y), grp: 16 (over z, x, core).
Axes of the slice: x: 2, y: 2, z: 4, core: 2. Of those that a mesh axis runs over, the one named last changes fastest.
Arguments:
- positions: float32 [3, 8192], P(None, ('blk', 'grp')), may hold values from -6 to 6
- velocities: float32 [3, 8192], P(None, ('blk', 'grp')), may hold values from -6 to 6
- accelerations: float32 [3, 8192], P(None, ('blk', 'grp')), may hold values from -4 to 4
- jerks: float32 [3, 8192], P(None, ('blk', 'grp')), may hold values from -4 to 4
- mass_weight: float32 [8192], P(('blk', 'grp')), may hold values from 0.3 to 3
- levels: int32 [8192], P(('blk', 'grp')), may hold values from 0 to 3, as said below
- active: int32 [2, 768], P(None, ('blk', 'grp')), may hold values from 0 to 255, as said below
- counts: int32 [2, 32], P(None, ('blk', 'grp')), may hold values from 1 to 24
Outputs:
- positions_out: float32 [3, 8192], P(None, ('blk', 'grp'))
- velocities_out: float32 [3, 8192], P(None, ('blk', 'grp'))
- accelerations_out: float32 [3, 8192], P(None, ('blk', 'grp'))
- jerks_out: float32 [3, 8192], P(None, ('blk', 'grp'))
- fresh_forces: float32 [2, 6, 768], P(None, None, ('blk', 'grp'))
The draws below stay inside these ranges and needn't reach their ends.
Inputs may be any that keep to these rules, and one draw needn't show every extreme that they name: `active`: entries are local indices of the owner's particles; the live slots of one owner's list are distinct, dead slots hold 0. `levels`: particles not named in any list have level 2 or 3.
All inputs are finite; a program needn't handle non-finite values.
Results may differ from the reference program's by a relative error of at most 0.0003.
Values sent between devices are 32-bit elements; how exact they have to be, the bound alone decides.
A program may use at most 64 MiB of HBM per device.

```python
import math
import jax
import jax.numpy as jnp
from jax import lax

PART_DEV = 256
ACT = 24
OWNERS = 32
NPART = 8192


def roster(key):
    load_key, full_key, first_key, order_key, rest_key = jax.random.split(jax.random.fold_in(key, 17), 5)
    owner_ids = jnp.arange(OWNERS, dtype=jnp.int32)
    busiest = jax.random.randint(full_key, (), 0, OWNERS)
    pair_ids = (owner_ids // 2).astype(jnp.int32)
    odd_owner = (owner_ids % 2).astype(jnp.int32)
    pair_draw = jax.random.randint(first_key, (OWNERS // 2,), 1, ACT).astype(jnp.int32)
    pair_slots = jnp.arange(OWNERS // 2, dtype=jnp.int32)
    pair_draw = jnp.where(pair_slots == busiest // 2, ACT - 1, pair_draw).astype(jnp.int32)
    even_first = pair_draw[pair_ids]
    first = jnp.where(odd_owner == 1, ACT - even_first, even_first).astype(jnp.int32)
    load = ACT - jax.random.randint(load_key, (OWNERS,), 0, ACT // 8 + 1)
    load = jnp.where(owner_ids == busiest, ACT, load).astype(jnp.int32)
    load = jnp.maximum(load, first).astype(jnp.int32)
    orders = jax.vmap(lambda k: jax.random.permutation(k, PART_DEV))(jax.random.split(order_key, OWNERS)).astype(jnp.int32)
    rank = jnp.arange(PART_DEV, dtype=jnp.int32)
    slower = 2 + jax.random.randint(rest_key, (OWNERS, PART_DEV), 0, 2)
    by_rank = jnp.where(rank[None, :] < first[:, None], 0, jnp.where(rank[None, :] < load[:, None], 1, slower)).astype(jnp.int32)
    empty = jnp.zeros((OWNERS, PART_DEV), jnp.int32)
    level_rows = jax.vmap(lambda row, order, value: row.at[order].set(value))(empty, orders, by_rank)
    slots = jnp.arange(ACT, dtype=jnp.int32)
    leading = orders[:, :ACT]
    step_one = jnp.where(slots[None, :] < first[:, None], leading, 0)
    step_two = jnp.where(slots[None, :] < load[:, None], leading, 0)
    lists = jnp.stack([step_one, step_two]).reshape(2, OWNERS * ACT).astype(jnp.int32)
    tallies = jnp.stack([first, load]).astype(jnp.int32)
    return (level_rows.reshape(OWNERS * PART_DEV).astype(jnp.int32), lists, tallies)


def draw_levels(key, part):
    return roster(key)[0]


def draw_active(key, part):
    return roster(key)[1]


def draw_counts(key, part):
    return roster(key)[2]


def block_scale(rng, shape, pieces, least, largest):
    loudness = 1.0
    for position, blocks in pieces:
        heights = jax.random.uniform(jax.random.fold_in(jax.random.fold_in(rng, 6), position), (blocks,), jnp.float32, least / len(pieces), largest / len(pieces))
        loudness = loudness * jnp.repeat(jnp.exp(heights), shape[position] // blocks).reshape((-1,) + (1,) * (len(shape) - 1 - position))
    return loudness


def scatter_about(key, extent, scale, most, cuts=(), kind=jnp.bfloat16):
    gain = block_scale(key, extent, cuts, -0.22, 0.18) if cuts else 1.0
    values = jax.random.normal(key, extent, jnp.float32) * scale * gain
    return jnp.minimum(jnp.maximum(values, -most), most).astype(kind)


def setup_inputs(seed: int = 0) -> dict:
    key_of = jax.random.split(jax.random.key(seed), 9)
    positions = scatter_about(key_of[0], (3, NPART), 1.0, 6.0, ((1, 32),), jnp.float32)
    velocities = scatter_about(key_of[1], (3, NPART), 1.0, 6.0, ((1, 32),), jnp.float32)
    accelerations = scatter_about(key_of[2], (3, NPART), 0.3, 4.0, ((1, 32),), jnp.float32)
    jerks = scatter_about(key_of[3], (3, NPART), 0.3, 4.0, ((1, 32),), jnp.float32)
    mass_weight = jnp.clip(jnp.exp(math.log(3.0) - 2.3025851 * jax.random.uniform(key_of[4], (NPART,), jnp.float32) ** block_scale(key_of[4], (NPART,), ((0, 32),), -0.2, 0.2)), 0.3, 3.0)
    levels = draw_levels(jax.random.fold_in(key_of[8], 71), 0)
    active = draw_active(jax.random.fold_in(key_of[8], 71), 0)
    counts = draw_counts(jax.random.fold_in(key_of[8], 71), 0)
    return dict(positions=positions, velocities=velocities, accelerations=accelerations, jerks=jerks, mass_weight=mass_weight, levels=levels, active=active, counts=counts)


STEP_BASE = 0.125
SOFTEN = 0.01

def predict(pos, vel, acc, jerk, elapsed):
    pred_pos = pos + elapsed * (vel + elapsed * (acc * 0.5 + elapsed * jerk / 6.0))
    pred_vel = vel + elapsed * (acc + elapsed * jerk * 0.5)
    return (pred_pos, pred_vel)

def correct(pos, vel, acc, jerk, new_acc, new_jerk, stride, hit):
    half = 0.5 * stride
    square = stride * stride / 12.0
    vel_new = vel + half * (acc + new_acc) + square * (jerk - new_jerk)
    pos_new = pos + half * (vel + vel_new) + square * (acc - new_acc)
    return (jnp.where(hit, pos_new, pos), jnp.where(hit, vel_new, vel), jnp.where(hit, new_acc, acc), jnp.where(hit, new_jerk, jerk))

def pair_terms(iblock, jpart):
    dpos = jpart[0:3, :, None] - iblock[0:3, None, :]
    dvel = jpart[3:6, :, None] - iblock[3:6, None, :]
    dist = dpos[0] * dpos[0] + dpos[1] * dpos[1] + dpos[2] * dpos[2] + SOFTEN
    inverse = lax.rsqrt(dist)
    weight = jpart[6][:, None] * inverse * inverse * inverse
    radial = 3.0 * (dpos[0] * dvel[0] + dpos[1] * dvel[1] + dpos[2] * dvel[2]) * inverse * inverse
    accel = lax.optimization_barrier(jnp.sum(weight[None] * dpos, axis=1))
    jerk = lax.optimization_barrier(jnp.sum(weight[None] * (dvel - radial[None] * dpos), axis=1))
    return jnp.concatenate([accel, jerk], axis=0)

def forces_all(chosen, jdata):
    rows = chosen.shape[1]
    width = 64
    blocks = chosen.reshape(6, rows // width, width).transpose(1, 0, 2)
    result = lax.map(lambda iblock: pair_terms(iblock, jdata), blocks)
    return result.transpose(1, 0, 2).reshape(6, rows)

def reference(positions, velocities, accelerations, jerks, mass_weight, levels, active, counts):
    mass = mass_weight / NPART
    clock = jnp.zeros((NPART,), jnp.float32)
    stride = STEP_BASE * jnp.left_shift(jnp.ones_like(levels), levels).astype(jnp.float32)
    slot = jnp.arange(OWNERS * ACT, dtype=jnp.int32)
    owner = (slot // ACT).astype(jnp.int32)
    global_index = (active + owner[None, :] * PART_DEV).astype(jnp.int32)
    pos, vel, acc, jerk = (positions, velocities, accelerations, jerks)
    recorded = []
    for step in range(2):
        now = STEP_BASE * (step + 1)
        elapsed = now - clock
        pred_pos, pred_vel = predict(pos, vel, acc, jerk, elapsed)
        live = slot % ACT < counts[step][owner]
        target = jnp.where(live, global_index[step], NPART).astype(jnp.int32)
        pred_both = jnp.concatenate([pred_pos, pred_vel], axis=0)
        chosen = pred_both[:, jnp.minimum(target, NPART - 1)]
        jdata = jnp.concatenate([pred_pos, pred_vel, mass[None, :]], axis=0)
        fresh = forces_all(chosen, jdata)
        recorded.append(jnp.where(live[None, :], fresh, jnp.zeros_like(fresh)))
        spread = jnp.zeros((6, NPART), jnp.float32).at[:, target].set(fresh, mode='drop')
        hit = jnp.zeros((NPART,), jnp.float32).at[target].set(1.0, mode='drop') > 0.5
        pos, vel, acc, jerk = correct(pos, vel, acc, jerk, spread[0:3], spread[3:6], stride, hit)
        clock = jnp.where(hit, now, clock)
    return (pos, vel, acc, jerk, jnp.stack(recorded))
```

```python
import functools
import math

import jax
import jax.numpy as jnp
from jax import lax
from jax.experimental import pallas as pl
from jax.experimental.pallas import tpu as pltpu
from jax.sharding import PartitionSpec as P

STEP_BASE = 0.125
SOFTEN = 0.01
LANES = 128
MESH = pl.DeviceIdType.MESH


def predict(pos, vel, acc, jerk, elapsed):
    pred_pos = pos + elapsed * (vel + elapsed * (acc * 0.5 + elapsed * jerk / 6.0))
    pred_vel = vel + elapsed * (acc + elapsed * jerk * 0.5)
    return (pred_pos, pred_vel)


def correct(pos, vel, acc, jerk, new_acc, new_jerk, stride, hit):
    half = 0.5 * stride
    square = stride * stride / 12.0
    vel_new = vel + half * (acc + new_acc) + square * (jerk - new_jerk)
    pos_new = pos + half * (vel + vel_new) + square * (acc - new_acc)
    return (
        jnp.where(hit, pos_new, pos),
        jnp.where(hit, vel_new, vel),
        jnp.where(hit, new_acc, acc),
        jnp.where(hit, new_jerk, jerk),
    )


def add_pairs(target, source, total):
    dpos = [source[c] - target[c] for c in range(3)]
    dvel = [source[c + 3] - target[c + 3] for c in range(3)]
    dist = dpos[0] * dpos[0] + dpos[1] * dpos[1] + dpos[2] * dpos[2] + SOFTEN
    inverse = lax.rsqrt(dist)
    square = inverse * inverse
    weight = source[6] * (inverse * square)
    radial = (3.0 * square) * (dpos[0] * dvel[0] + dpos[1] * dvel[1] + dpos[2] * dvel[2])
    accel = [total[c] + weight * dpos[c] for c in range(3)]
    jerk = [total[c + 3] + weight * (dvel[c] - radial * dpos[c]) for c in range(3)]
    return tuple(accel + jerk)


def kernel(
    n_blk, n_grp, act,
    pos_h, vel_h, acc_h, jerk_h, mass_h, lev_h, lists_h, counts_h,
    pos_o, vel_o, acc_o, jerk_o, fresh_o,
    pos_v, vel_v, acc_v, jerk_v, mass_v, lev_v, lists_v, counts_v,
    src1, src2, extra, tgt1, tgt2, part1, part2,
    load_sem, bulk_send, bulk_recv, pair_send, pair_recv,
):
    blk, grp = lax.axis_index("blk"), lax.axis_index("grp")
    per_blk = n_grp // 2
    chips = n_blk * per_blk
    core = lax.rem(grp, 2)
    chip = blk * per_blk + grp // 2
    partner = (blk, grp + 1 - 2 * core)
    part_dev = pos_h.shape[1]
    total_part = part_dev * n_blk * n_grp
    width = 1 << (act - 1).bit_length()
    group = math.gcd(LANES // width, chips)

    def chip_at(k):
        there = lax.rem(chip + k, chips)
        return (there // per_blk, 2 * lax.rem(there, per_blk) + core)

    loads = [
        pltpu.make_async_copy(h, v, load_sem.at[i])
        for i, (h, v) in enumerate(
            [(pos_h, pos_v), (vel_h, vel_v), (acc_h, acc_v), (jerk_h, jerk_v),
             (mass_h, mass_v), (lev_h, lev_v), (lists_h, lists_v), (counts_h, counts_v)]
        )
    ]
    for load in loads:
        load.start()

    barrier = pltpu.get_barrier_semaphore()

    def greet(k, carry):
        pl.semaphore_signal(barrier, inc=1, device_id=chip_at(k), device_id_type=MESH)
        return carry

    lax.fori_loop(1, chips, greet, 0)
    pl.semaphore_signal(barrier, inc=1, device_id=partner, device_id_type=MESH)

    def send_bulk(buffer, which):
        def send(k, carry):
            pltpu.make_async_remote_copy(
                src_ref=buffer.at[0], dst_ref=buffer.at[k],
                send_sem=bulk_send.at[which], recv_sem=bulk_recv.at[which],
                device_id=chip_at(k), device_id_type=MESH,
            ).start()
            return carry

        lax.fori_loop(1, chips, send, 0)

    def whole_bulk(buffer, which):
        others = buffer.at[pl.ds(1, chips - 1)]
        return pltpu.make_async_remote_copy(
            src_ref=others, dst_ref=others,
            send_sem=bulk_send.at[which], recv_sem=bulk_recv.at[which],
            device_id=partner, device_id_type=MESH,
        )

    def pair_copy(buffer, which):
        return pltpu.make_async_remote_copy(
            src_ref=buffer.at[0], dst_ref=buffer.at[1],
            send_sem=pair_send.at[which], recv_sem=pair_recv.at[which],
            device_id=partner, device_id_type=MESH,
        )

    for load in loads:
        load.wait()
    pos, vel, acc, jerk = pos_v[...], vel_v[...], acc_v[...], jerk_v[...]
    mass = mass_v[...] / total_part
    levels = lev_v[...]
    stride = STEP_BASE * jnp.left_shift(jnp.ones_like(levels), levels).astype(jnp.float32)
    hit_one, hit_two = levels == 0, levels <= 1
    pred_pos, pred_vel = predict(pos, vel, acc, jerk, STEP_BASE)
    src1[0, 0:3, :] = pred_pos
    src1[0, 3:6, :] = pred_vel
    src1[0, 6:7, :] = mass
    src1[0, 7:8, :] = jnp.zeros_like(mass)

    pl.semaphore_wait(barrier, chips)
    send_bulk(src1, 0)

    sub_row = lax.broadcasted_iota(jnp.int32, (act, LANES), 0)
    lane = lax.broadcasted_iota(jnp.int32, (act, LANES), 1)
    particle = lax.broadcasted_iota(jnp.int32, (act, part_dev), 1)
    count_one = jnp.broadcast_to(counts_v[0:1, :], (act, LANES))
    count_two = jnp.broadcast_to(counts_v[1:2, :], (act, LANES))
    list_one = jnp.concatenate([lists_v[0:1, :], jnp.zeros((1, LANES - act), jnp.int32)], axis=1)
    list_two = jnp.concatenate([lists_v[1:2, :], jnp.zeros((1, LANES - act), jnp.int32)], axis=1)
    shift = core * (act - count_one)
    place_one = (lane == sub_row - shift) & (lane < count_one)
    place_two = (lane == sub_row) & (lane < count_two)

    def picker_of(place, row):
        value = jnp.where(place, (row + 1).astype(jnp.float32), 0.0)
        column = jnp.sum(value, axis=1, keepdims=True) - 1.0
        return particle.astype(jnp.float32) == column

    def picked(picker, rows):
        return jnp.sum(jnp.where(picker, rows, 0.0), axis=1, keepdims=True)

    def packed(columns):
        tile = jnp.zeros((act, LANES), jnp.float32)
        for c, column in enumerate(columns):
            tile = jnp.where(lane == c, column, tile)
        return tile

    def spread(mask, tile):
        return [
            jnp.sum(jnp.where(mask, tile[:, c : c + 1], 0.0), axis=0, keepdims=True)
            for c in range(6)
        ]

    def targets_of(tile):
        return [jnp.broadcast_to(tile[:, c : c + 1], (act, LANES)) for c in range(6)]

    def zeros():
        return tuple(jnp.zeros((act, LANES), jnp.float32) for _ in range(6))

    def over_bulk(targets, buffer, total):
        def slot(k, total):
            for start in range(0, part_dev, LANES):
                rows = [buffer[k, c : c + 1, start : start + LANES] for c in range(7)]
                total = add_pairs(targets, rows, total)
            return total

        return lax.fori_loop(0, chips, slot, total)

    def over_extra(targets, total):
        def chunk(g, total):
            tile = extra[g * group]
            for i in range(1, group):
                tile = tile + extra[g * group + i]
            return add_pairs(targets, [tile[c : c + 1] for c in range(7)], total)

        return lax.fori_loop(0, chips // group, chunk, total)

    def reduced(total):
        return packed([jnp.sum(part, axis=1, keepdims=True) for part in total])

    picker_one = picker_of(place_one, list_one)
    tgt1[0] = packed(
        [picked(picker_one, pred_pos[c : c + 1]) for c in range(3)]
        + [picked(picker_one, pred_vel[c : c + 1]) for c in range(3)]
    )
    to_pair_one = pair_copy(tgt1, 0)
    to_pair_one.start()
    late_pos, late_vel = predict(pos, vel, acc, jerk, 2 * STEP_BASE)
    src2[0, 0:3, :] = late_pos
    src2[0, 3:6, :] = late_vel
    src2[0, 6:7, :] = jnp.where(hit_one, 0.0, mass)
    src2[0, 7:8, :] = jnp.zeros_like(mass)
    send_bulk(src2, 1)
    picker_two = picker_of(place_two, list_two)
    to_pair_one.wait_recv()
    targets = targets_of(tgt1[0] + tgt1[1])
    whole_bulk(src1, 0).wait_recv()
    part1[0] = reduced(over_bulk(targets, src1, zeros()))
    sums_one = pair_copy(part1, 1)
    sums_one.start()
    sums_one.wait_recv()
    force_one = part1[0] + part1[1]
    rows = spread(picker_one, force_one)
    new_acc, new_jerk = jnp.concatenate(rows[0:3], axis=0), jnp.concatenate(rows[3:6], axis=0)
    pos, vel, acc, jerk = correct(pos, vel, acc, jerk, new_acc, new_jerk, stride, hit_one)

    elapsed = jnp.where(hit_one, STEP_BASE, 2 * STEP_BASE)
    pred_pos, pred_vel = predict(pos, vel, acc, jerk, elapsed)
    columns = (
        [picked(picker_two, pred_pos[c : c + 1]) for c in range(3)]
        + [picked(picker_two, pred_vel[c : c + 1]) for c in range(3)]
        + [picked(picker_two, jnp.where(hit_one, mass, 0.0))]
    )
    offset = lax.rem(chip, group) * width
    window = lane == sub_row + offset
    for c, column in enumerate(columns):
        extra[0, c : c + 1, :] = jnp.sum(jnp.where(window, column, 0.0), axis=0, keepdims=True)
    extra[0, 7:8, :] = jnp.zeros((1, LANES), jnp.float32)
    send_bulk(extra, 2)
    tgt2[0] = packed(columns[0:6])
    to_pair_two = pair_copy(tgt2, 2)
    to_pair_two.start()
    for c, row in enumerate(spread(place_one, force_one)):
        fresh_o[0, c : c + 1, :] = row[:, 0:act]

    whole_bulk(src2, 1).wait_recv()
    own_total = over_bulk([jnp.broadcast_to(c, (act, LANES)) for c in columns[0:6]], src2, zeros())
    part2[2] = reduced(own_total)
    to_pair_two.wait_recv()
    targets = targets_of(tgt2[1])
    total = over_bulk(targets, src2, zeros())
    whole_bulk(extra, 2).wait_recv()
    part2[0] = reduced(over_extra(targets, total))
    sums_two = pair_copy(part2, 3)
    sums_two.start()
    own_extra = reduced(over_extra(targets_of(tgt2[0]), zeros()))
    own = part2[2] + own_extra
    sums_two.wait_recv()
    force_two = own + part2[1]
    rows = spread(picker_two, force_two)
    new_acc, new_jerk = jnp.concatenate(rows[0:3], axis=0), jnp.concatenate(rows[3:6], axis=0)
    pos, vel, acc, jerk = correct(pos, vel, acc, jerk, new_acc, new_jerk, stride, hit_two)
    pos_o[...] = pos
    vel_o[...] = vel
    acc_o[...] = acc
    jerk_o[...] = jerk
    for c, row in enumerate(spread(place_two, force_two)):
        fresh_o[1, c : c + 1, :] = row[:, 0:act]

    for which, buffer in enumerate((src1, src2, extra)):
        whole_bulk(buffer, which).wait_send()
    for copy in (to_pair_one, sums_one, to_pair_two, sums_two):
        copy.wait_send()


def body(n_blk, n_grp, positions, velocities, accelerations, jerks, mass_weight, levels, active, counts):
    part_dev, act = positions.shape[1], active.shape[1]
    chips = n_blk * n_grp // 2
    state = jax.ShapeDtypeStruct((3, part_dev), jnp.float32)
    vmem = pltpu.VMEM
    return pl.pallas_call(
        functools.partial(kernel, n_blk, n_grp, act),
        out_shape=(state, state, state, state, jax.ShapeDtypeStruct((2, 6, act), jnp.float32)),
        in_specs=[pl.BlockSpec(memory_space=pl.ANY)] * 8,
        out_specs=[pl.BlockSpec(memory_space=vmem)] * 5,
        scratch_shapes=[
            vmem((3, part_dev), jnp.float32),
            vmem((3, part_dev), jnp.float32),
            vmem((3, part_dev), jnp.float32),
            vmem((3, part_dev), jnp.float32),
            vmem((1, part_dev), jnp.float32),
            vmem((1, part_dev), jnp.int32),
            vmem((2, act), jnp.int32),
            vmem((2, 1), jnp.int32),
            vmem((chips, 8, part_dev), jnp.float32),
            vmem((chips, 8, part_dev), jnp.float32),
            vmem((chips, 8, LANES), jnp.float32),
            vmem((2, act, LANES), jnp.float32),
            vmem((2, act, LANES), jnp.float32),
            vmem((2, act, LANES), jnp.float32),
            vmem((3, act, LANES), jnp.float32),
            pltpu.SemaphoreType.DMA((8,)),
            pltpu.SemaphoreType.DMA((3,)),
            pltpu.SemaphoreType.DMA((3,)),
            pltpu.SemaphoreType.DMA((4,)),
            pltpu.SemaphoreType.DMA((4,)),
        ],
        compiler_params=pltpu.CompilerParams(
            collective_id=0, has_side_effects=True, vmem_limit_bytes=32 * 1024 * 1024
        ),
    )(
        positions, velocities, accelerations, jerks,
        mass_weight.reshape(1, part_dev), levels.reshape(1, part_dev), active, counts,
    )


def solution(mesh):
    spread_over = ("blk", "grp")
    in_specs = (
        P(None, spread_over),
        P(None, spread_over),
        P(None, spread_over),
        P(None, spread_over),
        P(spread_over),
        P(spread_over),
        P(None, spread_over),
        P(None, spread_over),
    )
    out_specs = (
        P(None, spread_over),
        P(None, spread_over),
        P(None, spread_over),
        P(None, spread_over),
        P(None, None, spread_over),
    )
    inner = functools.partial(body, mesh.shape["blk"], mesh.shape["grp"])
    return jax.shard_map(inner, mesh=mesh, in_specs=in_specs, out_specs=out_specs, check_vma=False)
```

```python
import functools
import math

import jax
import jax.numpy as jnp
from jax import lax
from jax.experimental import pallas as pl
from jax.experimental.pallas import tpu as pltpu
from jax.sharding import PartitionSpec as P

STEP_BASE = 0.125
SOFTEN = 0.01
LANES = 128
MESH = pl.DeviceIdType.MESH


def predict(pos, vel, acc, jerk, elapsed):
    pred_pos = pos + elapsed * (vel + elapsed * (acc * 0.5 + elapsed * jerk / 6.0))
    pred_vel = vel + elapsed * (acc + elapsed * jerk * 0.5)
    return (pred_pos, pred_vel)


def correct(pos, vel, acc, jerk, new_acc, new_jerk, stride, hit):
    half = 0.5 * stride
    square = stride * stride / 12.0
    vel_new = vel + half * (acc + new_acc) + square * (jerk - new_jerk)
    pos_new = pos + half * (vel + vel_new) + square * (acc - new_acc)
    return (
        jnp.where(hit, pos_new, pos),
        jnp.where(hit, vel_new, vel),
        jnp.where(hit, new_acc, acc),
        jnp.where(hit, new_jerk, jerk),
    )


def add_pairs(target, source, total):
    dpos = [source[c] - target[c] for c in range(3)]
    dvel = [source[c + 3] - target[c + 3] for c in range(3)]
    dist = dpos[0] * dpos[0] + dpos[1] * dpos[1] + dpos[2] * dpos[2] + SOFTEN
    inverse = lax.rsqrt(dist)
    square = inverse * inverse
    weight = source[6] * (inverse * square)
    radial = (3.0 * square) * (dpos[0] * dvel[0] + dpos[1] * dvel[1] + dpos[2] * dvel[2])
    accel = [total[c] + weight * dpos[c] for c in range(3)]
    jerk = [total[c + 3] + weight * (dvel[c] - radial * dpos[c]) for c in range(3)]
    return tuple(accel + jerk)


def kernel(
    n_blk, n_grp, act,
    pos_h, vel_h, acc_h, jerk_h, mass_h, lev_h, lists_h, counts_h,
    pos_o, vel_o, acc_o, jerk_o, fresh_o,
    pos_v, vel_v, acc_v, jerk_v, mass_v, lev_v, lists_v, counts_v,
    src1, src2, extra, tgt1, tgt2, part1, part2,
    load_sem, bulk_send, bulk_recv, pair_send, pair_recv,
):
    blk, grp = lax.axis_index("blk"), lax.axis_index("grp")
    per_blk = n_grp // 2
    chips = n_blk * per_blk
    core = lax.rem(grp, 2)
    chip = blk * per_blk + grp // 2
    partner = (blk, grp + 1 - 2 * core)
    part_dev = pos_h.shape[1]
    total_part = part_dev * n_blk * n_grp
    width = 1 << (act - 1).bit_length()
    group = math.gcd(LANES // width, chips)

    def chip_at(k):
        there = lax.rem(chip + k, chips)
        return (there // per_blk, 2 * lax.rem(there, per_blk) + core)

    loads = [
        pltpu.make_async_copy(h, v, load_sem.at[i])
        for i, (h, v) in enumerate(
            [(pos_h, pos_v), (vel_h, vel_v), (acc_h, acc_v), (jerk_h, jerk_v),
             (mass_h, mass_v), (lev_h, lev_v), (lists_h, lists_v), (counts_h, counts_v)]
        )
    ]

    barrier = pltpu.get_barrier_semaphore()

    def greet(k, carry):
        pl.semaphore_signal(barrier, inc=1, device_id=chip_at(k), device_id_type=MESH)
        return carry

    lax.fori_loop(1, chips, greet, 0)
    pl.semaphore_signal(barrier, inc=1, device_id=partner, device_id_type=MESH)
    for load in loads:
        load.start()

    def send_bulk(buffer, which):
        def send(k, carry):
            pltpu.make_async_remote_copy(
                src_ref=buffer.at[0], dst_ref=buffer.at[k],
                send_sem=bulk_send.at[which], recv_sem=bulk_recv.at[which, k // group],
                device_id=chip_at(k), device_id_type=MESH,
            ).start()
            return carry

        lax.fori_loop(1, chips, send, 0)

    def arrival(buffer, which, first, count, sems):
        others = buffer.at[pl.ds(first, count)]
        return pltpu.make_async_remote_copy(
            src_ref=others, dst_ref=others,
            send_sem=bulk_send.at[which], recv_sem=bulk_recv.at[which, sems],
            device_id=partner, device_id_type=MESH,
        )

    def await_group(buffer, which, g):
        if isinstance(g, int) and g == 0:
            if group > 1:
                arrival(buffer, which, 1, group - 1, 0).wait_recv()
        else:
            arrival(buffer, which, g * group, group, g).wait_recv()

    def pair_copy(buffer, which):
        return pltpu.make_async_remote_copy(
            src_ref=buffer.at[0], dst_ref=buffer.at[1],
            send_sem=pair_send.at[which], recv_sem=pair_recv.at[which],
            device_id=partner, device_id_type=MESH,
        )

    for load in loads:
        load.wait()
    pos, vel, acc, jerk = pos_v[...], vel_v[...], acc_v[...], jerk_v[...]
    mass = mass_v[...] / total_part
    levels = lev_v[...]
    stride = STEP_BASE * jnp.left_shift(jnp.ones_like(levels), levels).astype(jnp.float32)
    hit_one, hit_two = levels == 0, levels <= 1
    pred_pos, pred_vel = predict(pos, vel, acc, jerk, STEP_BASE)
    src1[0, 0:3, :] = pred_pos
    src1[0, 3:6, :] = pred_vel
    src1[0, 6:7, :] = mass
    src1[0, 7:8, :] = jnp.zeros_like(mass)

    sub_row = lax.broadcasted_iota(jnp.int32, (act, LANES), 0)
    lane = lax.broadcasted_iota(jnp.int32, (act, LANES), 1)
    particle = lax.broadcasted_iota(jnp.int32, (act, part_dev), 1)
    count_one = jnp.broadcast_to(counts_v[0:1, 0:1], (act, LANES))
    count_two = jnp.broadcast_to(counts_v[0:1, 1:2], (act, LANES))
    list_one = jnp.concatenate([lists_v[0:1, :], jnp.zeros((1, LANES - act), jnp.int32)], axis=1)
    list_two = jnp.concatenate([lists_v[1:2, :], jnp.zeros((1, LANES - act), jnp.int32)], axis=1)
    shift = core * (act - count_one)
    place_one = (lane == sub_row - shift) & (lane < count_one)
    place_two = (lane == sub_row) & (lane < count_two)

    def picker_of(place, row):
        value = jnp.where(place, (row + 1).astype(jnp.float32), 0.0)
        column = jnp.sum(value, axis=1, keepdims=True) - 1.0
        return particle.astype(jnp.float32) == column

    def picked(picker, rows):
        return jnp.sum(jnp.where(picker, rows, 0.0), axis=1, keepdims=True)

    def packed(columns):
        tile = jnp.zeros((act, LANES), jnp.float32)
        for c, column in enumerate(columns):
            tile = jnp.where(lane == c, column, tile)
        return tile

    def spread(mask, tile):
        return [
            jnp.sum(jnp.where(mask, tile[:, c : c + 1], 0.0), axis=0, keepdims=True)
            for c in range(6)
        ]

    def targets_of(tile):
        return [jnp.broadcast_to(tile[:, c : c + 1], (act, LANES)) for c in range(6)]

    def zeros():
        return tuple(jnp.zeros((act, LANES), jnp.float32) for _ in range(6))

    def over_bulk(targets, buffer, total, which=None):
        def some(g, total):
            if which is not None:
                await_group(buffer, which, g)
            for i in range(group):
                for start in range(0, part_dev, LANES):
                    k = g * group + i
                    rows = [buffer[k, c : c + 1, start : start + LANES] for c in range(7)]
                    total = add_pairs(targets, rows, total)
            return total

        return lax.fori_loop(1, chips // group, some, some(0, total))

    def over_extra(targets, total, which=None):
        def chunk(g, total):
            if which is not None:
                await_group(extra, which, g)
            tile = extra[g * group]
            for i in range(1, group):
                tile = tile + extra[g * group + i]
            return add_pairs(targets, [tile[c : c + 1] for c in range(7)], total)

        return lax.fori_loop(1, chips // group, chunk, chunk(0, total))

    def reduced(total):
        return packed([jnp.sum(part, axis=1, keepdims=True) for part in total])

    picker_one = picker_of(place_one, list_one)
    tgt1[0] = packed(
        [picked(picker_one, pred_pos[c : c + 1]) for c in range(3)]
        + [picked(picker_one, pred_vel[c : c + 1]) for c in range(3)]
    )
    late_pos, late_vel = predict(pos, vel, acc, jerk, 2 * STEP_BASE)
    src2[0, 0:3, :] = late_pos
    src2[0, 3:6, :] = late_vel
    src2[0, 6:7, :] = jnp.where(hit_one, 0.0, mass)
    src2[0, 7:8, :] = jnp.zeros_like(mass)
    picker_two = picker_of(place_two, list_two)
    pl.semaphore_wait(barrier, chips)
    to_pair_one = pair_copy(tgt1, 0)
    to_pair_one.start()
    send_bulk(src1, 0)
    send_bulk(src2, 1)
    to_pair_one.wait_recv()
    targets = targets_of(tgt1[0] + tgt1[1])
    part1[0] = reduced(over_bulk(targets, src1, zeros(), 0))
    sums_one = pair_copy(part1, 1)
    sums_one.start()
    sums_one.wait_recv()
    force_one = part1[0] + part1[1]
    rows = spread(picker_one, force_one)
    new_acc, new_jerk = jnp.concatenate(rows[0:3], axis=0), jnp.concatenate(rows[3:6], axis=0)
    pos, vel, acc, jerk = correct(pos, vel, acc, jerk, new_acc, new_jerk, stride, hit_one)

    elapsed = jnp.where(hit_one, STEP_BASE, 2 * STEP_BASE)
    pred_pos, pred_vel = predict(pos, vel, acc, jerk, elapsed)
    columns = (
        [picked(picker_two, pred_pos[c : c + 1]) for c in range(3)]
        + [picked(picker_two, pred_vel[c : c + 1]) for c in range(3)]
        + [picked(picker_two, jnp.where(hit_one, mass, 0.0))]
    )
    offset = lax.rem(chip, group) * width
    window = lane == sub_row + offset
    for c, column in enumerate(columns):
        extra[0, c : c + 1, :] = jnp.sum(jnp.where(window, column, 0.0), axis=0, keepdims=True)
    extra[0, 7:8, :] = jnp.zeros((1, LANES), jnp.float32)
    send_bulk(extra, 2)
    tgt2[0] = packed(columns[0:6])
    to_pair_two = pair_copy(tgt2, 2)
    to_pair_two.start()
    for c, row in enumerate(spread(place_one, force_one)):
        fresh_o[c, 0:1, :] = row[:, 0:act]

    own_total = over_bulk([jnp.broadcast_to(c, (act, LANES)) for c in columns[0:6]], src2, zeros(), 1)
    part2[2] = reduced(own_total)
    to_pair_two.wait_recv()
    targets = targets_of(tgt2[1])
    total = over_bulk(targets, src2, zeros())
    part2[0] = reduced(over_extra(targets, total, 2))
    sums_two = pair_copy(part2, 3)
    sums_two.start()
    own_extra = reduced(over_extra(targets_of(tgt2[0]), zeros()))
    own = part2[2] + own_extra
    sums_two.wait_recv()
    force_two = own + part2[1]
    rows = spread(picker_two, force_two)
    new_acc, new_jerk = jnp.concatenate(rows[0:3], axis=0), jnp.concatenate(rows[3:6], axis=0)
    pos, vel, acc, jerk = correct(pos, vel, acc, jerk, new_acc, new_jerk, stride, hit_two)
    pos_o[...] = pos
    vel_o[...] = vel
    acc_o[...] = acc
    jerk_o[...] = jerk
    for c, row in enumerate(spread(place_two, force_two)):
        fresh_o[c, 1:2, :] = row[:, 0:act]

    for which, buffer in enumerate((src1, src2, extra)):
        arrival(buffer, which, 1, chips - 1, 0).wait_send()
    for copy in (to_pair_one, sums_one, to_pair_two, sums_two):
        copy.wait_send()


def write_out(*refs):
    sems = refs[10]
    copies = [pltpu.make_async_copy(refs[i], refs[5 + i], sems.at[i]) for i in range(5)]
    for copy in copies:
        copy.start()
    for copy in copies:
        copy.wait()


def body(n_blk, n_grp, positions, velocities, accelerations, jerks, mass_weight, levels, active, counts):
    part_dev, act = positions.shape[1], active.shape[1]
    chips = n_blk * n_grp // 2
    state = pltpu.VMEM((3, part_dev), jnp.float32)
    vmem = pltpu.VMEM
    results = pl.pallas_call(
        functools.partial(kernel, n_blk, n_grp, act),
        out_shape=(state, state, state, state, pltpu.VMEM((6, 2, act), jnp.float32)),
        in_specs=[pl.BlockSpec(memory_space=pltpu.HBM)] * 8,
        out_specs=[pl.BlockSpec(memory_space=vmem)] * 5,
        scratch_shapes=[
            vmem((3, part_dev), jnp.float32),
            vmem((3, part_dev), jnp.float32),
            vmem((3, part_dev), jnp.float32),
            vmem((3, part_dev), jnp.float32),
            vmem((1, part_dev), jnp.float32),
            vmem((1, part_dev), jnp.int32),
            vmem((2, act), jnp.int32),
            vmem((1, 2), jnp.int32),
            vmem((chips, 8, part_dev), jnp.float32),
            vmem((chips, 8, part_dev), jnp.float32),
            vmem((chips, 8, LANES), jnp.float32),
            vmem((2, act, LANES), jnp.float32),
            vmem((2, act, LANES), jnp.float32),
            vmem((2, act, LANES), jnp.float32),
            vmem((3, act, LANES), jnp.float32),
            pltpu.SemaphoreType.DMA((8,)),
            pltpu.SemaphoreType.DMA((3,)),
            pltpu.SemaphoreType.DMA((3, chips)),
            pltpu.SemaphoreType.DMA((4,)),
            pltpu.SemaphoreType.DMA((4,)),
        ],
        compiler_params=pltpu.CompilerParams(
            collective_id=0, has_side_effects=True, vmem_limit_bytes=32 * 1024 * 1024
        ),
    )(*[pltpu.with_memory_space_constraint(value, pltpu.HBM) for value in (
        positions, velocities, accelerations, jerks,
        mass_weight.reshape(1, part_dev), levels.reshape(1, part_dev), active, counts.reshape(1, 2),
    )])
    written = pl.pallas_call(
        write_out,
        out_shape=[jax.ShapeDtypeStruct(r.shape, r.dtype) for r in results],
        in_specs=[pl.BlockSpec(memory_space=vmem)] * 5,
        out_specs=[pl.BlockSpec(memory_space=pltpu.HBM)] * 5,
        scratch_shapes=[pltpu.SemaphoreType.DMA((5,))],
    )(*results)
    return (*written[0:4], written[4].transpose(1, 0, 2))


def solution(mesh):
    spread_over = ("blk", "grp")
    in_specs = (
        P(None, spread_over),
        P(None, spread_over),
        P(None, spread_over),
        P(None, spread_over),
        P(spread_over),
        P(spread_over),
        P(None, spread_over),
        P(None, spread_over),
    )
    out_specs = (
        P(None, spread_over),
        P(None, spread_over),
        P(None, spread_over),
        P(None, spread_over),
        P(None, None, spread_over),
    )
    inner = functools.partial(body, mesh.shape["blk"], mesh.shape["grp"])
    return jax.shard_map(inner, mesh=mesh, in_specs=in_specs, out_specs=out_specs, check_vma=False)
```

```python
import functools
import math

import jax
import jax.numpy as jnp
from jax import lax
from jax.experimental import pallas as pl
from jax.experimental.pallas import tpu as pltpu
from jax.sharding import PartitionSpec as P

STEP_BASE = 0.125
SOFTEN = 0.01
LANES = 128
MESH = pl.DeviceIdType.MESH


def predict(pos, vel, acc, jerk, elapsed):
    pred_pos = pos + elapsed * (vel + elapsed * (acc * 0.5 + elapsed * jerk / 6.0))
    pred_vel = vel + elapsed * (acc + elapsed * jerk * 0.5)
    return (pred_pos, pred_vel)


def correct(pos, vel, acc, jerk, new_acc, new_jerk, stride, hit):
    half = 0.5 * stride
    square = stride * stride / 12.0
    vel_new = vel + half * (acc + new_acc) + square * (jerk - new_jerk)
    pos_new = pos + half * (vel + vel_new) + square * (acc - new_acc)
    return (
        jnp.where(hit, pos_new, pos),
        jnp.where(hit, vel_new, vel),
        jnp.where(hit, new_acc, acc),
        jnp.where(hit, new_jerk, jerk),
    )


def add_pairs(target, source, total):
    dpos = [source[c] - target[c] for c in range(3)]
    dvel = [source[c + 3] - target[c + 3] for c in range(3)]
    dist = dpos[0] * dpos[0] + dpos[1] * dpos[1] + dpos[2] * dpos[2] + SOFTEN
    inverse = lax.rsqrt(dist)
    square = inverse * inverse
    weight = source[6] * (inverse * square)
    radial = (3.0 * square) * (dpos[0] * dvel[0] + dpos[1] * dvel[1] + dpos[2] * dvel[2])
    accel = [total[c] + weight * dpos[c] for c in range(3)]
    jerk = [total[c + 3] + weight * (dvel[c] - radial * dpos[c]) for c in range(3)]
    return tuple(accel + jerk)


def kernel(
    n_blk, n_grp, act,
    pos_h, vel_h, acc_h, jerk_h, mass_h, lev_h, lists_h, counts_h,
    pos_o, vel_o, acc_o, jerk_o, fresh_o,
    pos_v, vel_v, acc_v, jerk_v, mass_v, lev_v, lists_v, counts_v,
    src1, src2, extra, tgt1, tgt2, part1, part2,
    load_sem, bulk_send, bulk_recv, pair_send, pair_recv,
):
    blk, grp = lax.axis_index("blk"), lax.axis_index("grp")
    per_blk = n_grp // 2
    chips = n_blk * per_blk
    core = lax.rem(grp, 2)
    chip = blk * per_blk + grp // 2
    partner = (blk, grp + 1 - 2 * core)
    part_dev = pos_h.shape[1]
    total_part = part_dev * n_blk * n_grp
    width = 1 << (act - 1).bit_length()
    group = math.gcd(LANES // width, chips)

    def device_at(there, which_core):
        return (there // per_blk, 2 * lax.rem(there, per_blk) + which_core)

    def far_first(visit):
        def turn(j, carry):
            step = ((j + 1) // 2) * (1 - 2 * lax.rem(j, 2))
            there = lax.rem(3 * chips - 1 + step - chip, chips)
            visit(there, lax.rem(there - chip + chips, chips))
            return carry

        lax.fori_loop(0, chips, turn, 0)

    loads = [
        pltpu.make_async_copy(h, v, load_sem.at[i])
        for i, (h, v) in enumerate(
            [(pos_h, pos_v), (vel_h, vel_v), (acc_h, acc_v), (jerk_h, jerk_v),
             (mass_h, mass_v), (lev_h, lev_v), (lists_h, lists_v), (counts_h, counts_v)]
        )
    ]

    barrier = pltpu.get_barrier_semaphore()

    def greet(there, k):
        def signal(which_core):
            pl.semaphore_signal(barrier, inc=1, device_id=device_at(there, which_core), device_id_type=MESH)

        pl.when(k != 0)(lambda: signal(core))
        signal(1 - core)

    far_first(greet)
    for load in loads:
        load.start()

    def send_bulk(buffer, which):
        def send(there, k):
            @pl.when(k != 0)
            def _():
                pltpu.make_async_remote_copy(
                    src_ref=buffer.at[0], dst_ref=buffer.at[k],
                    send_sem=bulk_send.at[which], recv_sem=bulk_recv.at[which, k // group],
                    device_id=device_at(there, core), device_id_type=MESH,
                ).start()

        far_first(send)

    def send_extra():
        def send(there, k):
            def copy(slot, which_core):
                pltpu.make_async_remote_copy(
                    src_ref=extra.at[0], dst_ref=extra.at[slot],
                    send_sem=bulk_send.at[2], recv_sem=bulk_recv.at[2, 0],
                    device_id=device_at(there, which_core), device_id_type=MESH,
                ).start()

            pl.when(k != 0)(lambda: copy(k, core))
            copy(chips + k, 1 - core)

        far_first(send)

    def arrival(buffer, which, first, count, sems):
        others = buffer.at[pl.ds(first, count)]
        return pltpu.make_async_remote_copy(
            src_ref=others, dst_ref=others,
            send_sem=bulk_send.at[which], recv_sem=bulk_recv.at[which, sems],
            device_id=partner, device_id_type=MESH,
        )

    def await_group(buffer, which, g):
        if isinstance(g, int) and g == 0:
            if group > 1:
                arrival(buffer, which, 1, group - 1, 0).wait_recv()
        else:
            arrival(buffer, which, g * group, group, g).wait_recv()

    def pair_copy(buffer, which):
        return pltpu.make_async_remote_copy(
            src_ref=buffer.at[0], dst_ref=buffer.at[1],
            send_sem=pair_send.at[which], recv_sem=pair_recv.at[which],
            device_id=partner, device_id_type=MESH,
        )

    for load in loads:
        load.wait()
    pos, vel, acc, jerk = pos_v[...], vel_v[...], acc_v[...], jerk_v[...]
    mass = mass_v[...] / total_part
    levels = lev_v[...]
    stride = STEP_BASE * jnp.left_shift(jnp.ones_like(levels), levels).astype(jnp.float32)
    hit_one, hit_two = levels == 0, levels <= 1
    pred_pos, pred_vel = predict(pos, vel, acc, jerk, STEP_BASE)
    src1[0, 0:3, :] = pred_pos
    src1[0, 3:6, :] = pred_vel
    src1[0, 6:7, :] = mass
    src1[0, 7:8, :] = jnp.zeros_like(mass)

    sub_row = lax.broadcasted_iota(jnp.int32, (act, LANES), 0)
    lane = lax.broadcasted_iota(jnp.int32, (act, LANES), 1)
    particle = lax.broadcasted_iota(jnp.int32, (act, part_dev), 1)
    count_one = jnp.broadcast_to(counts_v[0:1, 0:1], (act, LANES))
    count_two = jnp.broadcast_to(counts_v[0:1, 1:2], (act, LANES))
    list_one = jnp.concatenate([lists_v[0:1, :], jnp.zeros((1, LANES - act), jnp.int32)], axis=1)
    list_two = jnp.concatenate([lists_v[1:2, :], jnp.zeros((1, LANES - act), jnp.int32)], axis=1)
    shift = core * (act - count_one)
    place_one = (lane == sub_row - shift) & (lane < count_one)
    place_two = (lane == sub_row) & (lane < count_two)

    def picker_of(place, row):
        value = jnp.where(place, (row + 1).astype(jnp.float32), 0.0)
        column = jnp.sum(value, axis=1, keepdims=True) - 1.0
        return particle.astype(jnp.float32) == column

    def picked(picker, rows):
        return jnp.sum(jnp.where(picker, rows, 0.0), axis=1, keepdims=True)

    def packed(columns):
        tile = jnp.zeros((act, LANES), jnp.float32)
        for c, column in enumerate(columns):
            tile = jnp.where(lane == c, column, tile)
        return tile

    def spread(mask, tile):
        return [
            jnp.sum(jnp.where(mask, tile[:, c : c + 1], 0.0), axis=0, keepdims=True)
            for c in range(6)
        ]

    def targets_of(tile):
        return [jnp.broadcast_to(tile[:, c : c + 1], (act, LANES)) for c in range(6)]

    def zeros():
        return tuple(jnp.zeros((act, LANES), jnp.float32) for _ in range(6))

    def over_bulk(targets, buffer, total, which=None):
        def some(g, total):
            if which is not None:
                await_group(buffer, which, g)
            for i in range(group):
                for start in range(0, part_dev, LANES):
                    k = g * group + i
                    rows = [buffer[k, c : c + 1, start : start + LANES] for c in range(7)]
                    total = add_pairs(targets, rows, total)
            return total

        return lax.fori_loop(1, chips // group, some, some(0, total))

    blocks = LANES // width
    block = lax.broadcasted_iota(jnp.int32, (2, LANES), 1) // width
    first_block = [lax.rem(chip - i + 4 * chips, group) for i in range(group)]
    masks = [[block == lax.rem(q + first_block[i], blocks) for i in range(group)] for q in range(4)]

    def over_extra(targets, total):
        groups = 2 * chips // group
        batch = math.gcd(4, groups)

        def some(b, total):
            for g in range(batch):
                slots = [extra[(b * batch + g) * group + i] for i in range(group)]
                rows = [None] * 8
                for q in range(4):
                    both = jnp.where(masks[q][0], slots[0], 0.0)
                    for i in range(1, group):
                        both = jnp.where(masks[q][i], slots[i], both)
                    if q > 0:
                        both = pltpu.roll(both, LANES - q * width, 1)
                    rows[q], rows[q + 4] = both[0:1], both[1:2]
                total = add_pairs(targets, rows, total)
            return total

        return lax.fori_loop(0, groups // batch, some, total)

    def reduced(total):
        return packed([jnp.sum(part, axis=1, keepdims=True) for part in total])

    picker_one = picker_of(place_one, list_one)
    tgt1[0] = packed(
        [picked(picker_one, pred_pos[c : c + 1]) for c in range(3)]
        + [picked(picker_one, pred_vel[c : c + 1]) for c in range(3)]
    )
    late_pos, late_vel = predict(pos, vel, acc, jerk, 2 * STEP_BASE)
    src2[0, 0:3, :] = late_pos
    src2[0, 3:6, :] = late_vel
    src2[0, 6:7, :] = jnp.where(hit_one, 0.0, mass)
    src2[0, 7:8, :] = jnp.zeros_like(mass)
    picker_two = picker_of(place_two, list_two)
    window = lane == sub_row + lax.rem(chip, group) * width

    def in_slots(column):
        return jnp.sum(jnp.where(window, column, 0.0), axis=0, keepdims=True)

    slot_state = [
        [in_slots(picked(picker_one, rows[c : c + 1])) for c in range(3)]
        for rows in (pos, vel, acc, jerk)
    ]
    slot_mass = in_slots(picked(picker_one, mass))
    pl.semaphore_wait(barrier, 2 * chips - 1)
    to_pair_one = pair_copy(tgt1, 0)
    to_pair_one.start()
    send_bulk(src1, 0)
    send_bulk(src2, 1)
    to_pair_one.wait_recv()
    targets = targets_of(tgt1[0] + tgt1[1])
    part1[0] = reduced(over_bulk(targets, src1, zeros(), 0))
    sums_one = pair_copy(part1, 1)
    sums_one.start()
    sums_one.wait_recv()
    force_one = part1[0] + part1[1]

    rows = spread(window, force_one)
    moved = [None] * 8
    for c in range(3):
        state = correct(
            slot_state[0][c], slot_state[1][c], slot_state[2][c], slot_state[3][c],
            rows[c], rows[c + 3], STEP_BASE, True,
        )
        moved[c], moved[c + 3] = predict(*state, STEP_BASE)
    moved[6], moved[7] = slot_mass, jnp.zeros_like(slot_mass)
    for r in range(2):
        line = moved[4 * r]
        for q in range(1, 4):
            line = line + pltpu.roll(jnp.broadcast_to(moved[4 * r + q], (8, LANES)), q * width, 1)[0:1]
        extra[0, r : r + 1, :] = line
    send_extra()

    rows = spread(picker_one, force_one)
    new_acc, new_jerk = jnp.concatenate(rows[0:3], axis=0), jnp.concatenate(rows[3:6], axis=0)
    pos, vel, acc, jerk = correct(pos, vel, acc, jerk, new_acc, new_jerk, stride, hit_one)

    elapsed = jnp.where(hit_one, STEP_BASE, 2 * STEP_BASE)
    pred_pos, pred_vel = predict(pos, vel, acc, jerk, elapsed)
    tgt2[0] = packed(
        [picked(picker_two, pred_pos[c : c + 1]) for c in range(3)]
        + [picked(picker_two, pred_vel[c : c + 1]) for c in range(3)]
    )
    to_pair_two = pair_copy(tgt2, 2)
    to_pair_two.start()
    for c, row in enumerate(spread(place_one, force_one)):
        fresh_o[c, 0:1, :] = row[:, 0:act]
    own_targets = targets_of(tgt2[0])
    own_total = over_bulk(own_targets, src2, zeros(), 1)
    to_pair_two.wait_recv()
    part2[0] = reduced(over_bulk(targets_of(tgt2[1]), src2, zeros()))
    sums_two = pair_copy(part2, 3)
    sums_two.start()
    others = extra.at[pl.ds(1, 2 * chips - 1)]
    all_extra = pltpu.make_async_remote_copy(
        src_ref=others, dst_ref=others,
        send_sem=bulk_send.at[2], recv_sem=bulk_recv.at[2, 0],
        device_id=partner, device_id_type=MESH,
    )
    all_extra.wait_recv()
    own = reduced(over_extra(own_targets, own_total))
    sums_two.wait_recv()
    force_two = own + part2[1]
    rows = spread(picker_two, force_two)
    new_acc, new_jerk = jnp.concatenate(rows[0:3], axis=0), jnp.concatenate(rows[3:6], axis=0)
    pos, vel, acc, jerk = correct(pos, vel, acc, jerk, new_acc, new_jerk, stride, hit_two)
    pos_o[...] = pos
    vel_o[...] = vel
    acc_o[...] = acc
    jerk_o[...] = jerk
    for c, row in enumerate(spread(place_two, force_two)):
        fresh_o[c, 1:2, :] = row[:, 0:act]

    all_extra.wait_send()
    for which, buffer in enumerate((src1, src2)):
        arrival(buffer, which, 1, chips - 1, 0).wait_send()
    for copy in (to_pair_one, sums_one, to_pair_two, sums_two):
        copy.wait_send()


def write_out(*refs):
    sems = refs[10]
    copies = [pltpu.make_async_copy(refs[i], refs[5 + i], sems.at[i]) for i in range(5)]
    for copy in copies:
        copy.start()
    for copy in copies:
        copy.wait()


def body(n_blk, n_grp, positions, velocities, accelerations, jerks, mass_weight, levels, active, counts):
    part_dev, act = positions.shape[1], active.shape[1]
    chips = n_blk * n_grp // 2
    state = pltpu.VMEM((3, part_dev), jnp.float32)
    vmem = pltpu.VMEM
    results = pl.pallas_call(
        functools.partial(kernel, n_blk, n_grp, act),
        out_shape=(state, state, state, state, pltpu.VMEM((6, 2, act), jnp.float32)),
        in_specs=[pl.BlockSpec(memory_space=pltpu.HBM)] * 8,
        out_specs=[pl.BlockSpec(memory_space=vmem)] * 5,
        scratch_shapes=[
            vmem((3, part_dev), jnp.float32),
            vmem((3, part_dev), jnp.float32),
            vmem((3, part_dev), jnp.float32),
            vmem((3, part_dev), jnp.float32),
            vmem((1, part_dev), jnp.float32),
            vmem((1, part_dev), jnp.int32),
            vmem((2, act), jnp.int32),
            vmem((1, 2), jnp.int32),
            vmem((chips, 8, part_dev), jnp.float32),
            vmem((chips, 8, part_dev), jnp.float32),
            vmem((2 * chips, 2, LANES), jnp.float32),
            vmem((2, act, LANES), jnp.float32),
            vmem((2, act, LANES), jnp.float32),
            vmem((2, act, LANES), jnp.float32),
            vmem((2, act, LANES), jnp.float32),
            pltpu.SemaphoreType.DMA((8,)),
            pltpu.SemaphoreType.DMA((3,)),
            pltpu.SemaphoreType.DMA((3, chips)),
            pltpu.SemaphoreType.DMA((4,)),
            pltpu.SemaphoreType.DMA((4,)),
        ],
        compiler_params=pltpu.CompilerParams(
            collective_id=0, has_side_effects=True, vmem_limit_bytes=32 * 1024 * 1024
        ),
    )(*[pltpu.with_memory_space_constraint(value, pltpu.HBM) for value in (
        positions, velocities, accelerations, jerks,
        mass_weight.reshape(1, part_dev), levels.reshape(1, part_dev), active, counts.reshape(1, 2),
    )])
    written = pl.pallas_call(
        write_out,
        out_shape=[jax.ShapeDtypeStruct(r.shape, r.dtype) for r in results],
        in_specs=[pl.BlockSpec(memory_space=vmem)] * 5,
        out_specs=[pl.BlockSpec(memory_space=pltpu.HBM)] * 5,
        scratch_shapes=[pltpu.SemaphoreType.DMA((5,))],
        compiler_params=pltpu.CompilerParams(vmem_limit_bytes=1024 * 1024),
    )(*[pltpu.with_memory_space_constraint(value, vmem) for value in results])
    return (*written[0:4], written[4].transpose(1, 0, 2))


def solution(mesh):
    spread_over = ("blk", "grp")
    in_specs = (
        P(None, spread_over),
        P(None, spread_over),
        P(None, spread_over),
        P(None, spread_over),
        P(spread_over),
        P(spread_over),
        P(None, spread_over),
        P(None, spread_over),
    )
    out_specs = (
        P(None, spread_over),
        P(None, spread_over),
        P(None, spread_over),
        P(None, spread_over),
        P(None, None, spread_over),
    )
    inner = functools.partial(body, mesh.shape["blk"], mesh.shape["grp"])
    return jax.shard_map(inner, mesh=mesh, in_specs=in_specs, out_specs=out_specs, check_vma=False)
```

```python
import functools
import math

import jax
import jax.numpy as jnp
from jax import lax
from jax.experimental import pallas as pl
from jax.experimental.pallas import tpu as pltpu
from jax.sharding import PartitionSpec as P

STEP_BASE = 0.125
SOFTEN = 0.01
LANES = 128
MESH = pl.DeviceIdType.MESH


def predict(pos, vel, acc, jerk, elapsed):
    pred_pos = pos + elapsed * (vel + elapsed * (acc * 0.5 + elapsed * jerk / 6.0))
    pred_vel = vel + elapsed * (acc + elapsed * jerk * 0.5)
    return (pred_pos, pred_vel)


def correct(pos, vel, acc, jerk, new_acc, new_jerk, stride, hit):
    half = 0.5 * stride
    square = stride * stride / 12.0
    vel_new = vel + half * (acc + new_acc) + square * (jerk - new_jerk)
    pos_new = pos + half * (vel + vel_new) + square * (acc - new_acc)
    return (
        jnp.where(hit, pos_new, pos),
        jnp.where(hit, vel_new, vel),
        jnp.where(hit, new_acc, acc),
        jnp.where(hit, new_jerk, jerk),
    )


def add_pairs(target, source, total):
    dpos = [source[c] - target[c] for c in range(3)]
    dvel = [source[c + 3] - target[c + 3] for c in range(3)]
    dist = dpos[0] * dpos[0] + dpos[1] * dpos[1] + dpos[2] * dpos[2] + SOFTEN
    inverse = lax.rsqrt(dist)
    square = inverse * inverse
    weight = source[6] * (inverse * square)
    radial = (3.0 * square) * (dpos[0] * dvel[0] + dpos[1] * dvel[1] + dpos[2] * dvel[2])
    accel = [total[c] + weight * dpos[c] for c in range(3)]
    jerk = [total[c + 3] + weight * (dvel[c] - radial * dpos[c]) for c in range(3)]
    return tuple(accel + jerk)


def kernel(
    n_blk, n_grp, act,
    pos_h, vel_h, acc_h, jerk_h, mass_h, lev_h, lists_h, counts_h,
    pos_o, vel_o, acc_o, jerk_o, fresh_o,
    pos_v, vel_v, acc_v, jerk_v, mass_v, lev_v, lists_v, counts_v,
    src1, src2, extra, tgt1, tgt2, part1, part2,
    load_sem, bulk_send, bulk_recv, pair_send, pair_recv,
):
    blk, grp = lax.axis_index("blk"), lax.axis_index("grp")
    per_blk = n_grp // 2
    chips = n_blk * per_blk
    core = lax.rem(grp, 2)
    chip = blk * per_blk + grp // 2
    partner = (blk, grp + 1 - 2 * core)
    part_dev = pos_h.shape[1]
    total_part = part_dev * n_blk * n_grp
    width = 1 << (act - 1).bit_length()
    group = math.gcd(LANES // width, chips)

    def device_at(there, which_core):
        return (there // per_blk, 2 * lax.rem(there, per_blk) + which_core)

    def far_first(visit):
        def turn(j, carry):
            step = ((j + 1) // 2) * (1 - 2 * lax.rem(j, 2))
            there = lax.rem(3 * chips - 1 + step - chip, chips)
            visit(there, lax.rem(there - chip + chips, chips))
            return carry

        lax.fori_loop(0, chips, turn, 0)

    loads = [
        pltpu.make_async_copy(h, v, load_sem.at[i])
        for i, (h, v) in enumerate(
            [(pos_h, pos_v), (vel_h, vel_v), (acc_h, acc_v), (jerk_h, jerk_v),
             (mass_h, mass_v), (lev_h, lev_v), (lists_h, lists_v), (counts_h, counts_v)]
        )
    ]

    barrier = pltpu.get_barrier_semaphore()

    def greet(there, k):
        def signal(which_core):
            pl.semaphore_signal(barrier, inc=1, device_id=device_at(there, which_core), device_id_type=MESH)

        pl.when(k != 0)(lambda: signal(core))
        signal(1 - core)

    far_first(greet)
    for load in loads:
        load.start()

    def send_bulk(buffer, which):
        def send(there, k):
            @pl.when(k != 0)
            def _():
                pltpu.make_async_remote_copy(
                    src_ref=buffer.at[0], dst_ref=buffer.at[k],
                    send_sem=bulk_send.at[which], recv_sem=bulk_recv.at[which, k // group],
                    device_id=device_at(there, core), device_id_type=MESH,
                ).start()

        far_first(send)

    def send_extra():
        def send(there, k):
            def copy(half, which_core):
                pltpu.make_async_remote_copy(
                    src_ref=extra.at[0], dst_ref=extra.at[half * chips + k],
                    send_sem=bulk_send.at[2], recv_sem=bulk_recv.at[2 + half, k // group],
                    device_id=device_at(there, which_core), device_id_type=MESH,
                ).start()

            pl.when(k != 0)(lambda: copy(0, core))
            copy(1, 1 - core)

        far_first(send)

    def arrival(buffer, which, first, count, sems):
        others = buffer.at[pl.ds(first, count)]
        return pltpu.make_async_remote_copy(
            src_ref=others, dst_ref=others,
            send_sem=bulk_send.at[which], recv_sem=bulk_recv.at[which, sems],
            device_id=partner, device_id_type=MESH,
        )

    def await_group(buffer, which, g):
        if isinstance(g, int) and g == 0:
            if group > 1:
                arrival(buffer, which, 1, group - 1, 0).wait_recv()
        else:
            arrival(buffer, which, g * group, group, g).wait_recv()

    def pair_copy(buffer, which):
        return pltpu.make_async_remote_copy(
            src_ref=buffer.at[0], dst_ref=buffer.at[1],
            send_sem=pair_send.at[which], recv_sem=pair_recv.at[which],
            device_id=partner, device_id_type=MESH,
        )

    for load in loads:
        load.wait()
    pos, vel, acc, jerk = pos_v[...], vel_v[...], acc_v[...], jerk_v[...]
    mass = mass_v[...] / total_part
    levels = lev_v[...]
    stride = STEP_BASE * jnp.left_shift(jnp.ones_like(levels), levels).astype(jnp.float32)
    hit_one, hit_two = levels == 0, levels <= 1
    pred_pos, pred_vel = predict(pos, vel, acc, jerk, STEP_BASE)
    src1[0, 0:3, :] = pred_pos
    src1[0, 3:6, :] = pred_vel
    src1[0, 6:7, :] = mass
    src1[0, 7:8, :] = jnp.zeros_like(mass)

    sub_row = lax.broadcasted_iota(jnp.int32, (act, LANES), 0)
    lane = lax.broadcasted_iota(jnp.int32, (act, LANES), 1)
    particle = lax.broadcasted_iota(jnp.int32, (act, part_dev), 1)
    count_one = jnp.broadcast_to(counts_v[0:1, 0:1], (act, LANES))
    count_two = jnp.broadcast_to(counts_v[0:1, 1:2], (act, LANES))
    list_one = jnp.concatenate([lists_v[0:1, :], jnp.zeros((1, LANES - act), jnp.int32)], axis=1)
    list_two = jnp.concatenate([lists_v[1:2, :], jnp.zeros((1, LANES - act), jnp.int32)], axis=1)
    shift = core * (act - count_one)
    place_one = (lane == sub_row - shift) & (lane < count_one)
    place_two = (lane == sub_row) & (lane < count_two)

    def picker_of(place, row):
        value = jnp.where(place, (row + 1).astype(jnp.float32), 0.0)
        column = jnp.sum(value, axis=1, keepdims=True) - 1.0
        return particle.astype(jnp.float32) == column

    def picked(picker, rows):
        return jnp.sum(jnp.where(picker, rows, 0.0), axis=1, keepdims=True)

    def packed(columns):
        tile = jnp.zeros((act, LANES), jnp.float32)
        for c, column in enumerate(columns):
            tile = jnp.where(lane == c, column, tile)
        return tile

    def spread_columns(mask, columns):
        return [jnp.sum(jnp.where(mask, column, 0.0), axis=0, keepdims=True) for column in columns]

    def spread(mask, tile):
        return spread_columns(mask, [tile[:, c : c + 1] for c in range(6)])

    def targets_of(tile):
        return [jnp.broadcast_to(tile[:, c : c + 1], (act, LANES)) for c in range(6)]

    def zeros():
        return tuple(jnp.zeros((act, LANES), jnp.float32) for _ in range(6))

    def over_bulk(targets, buffer, total, which=None):
        def some(g, total):
            if which is not None:
                await_group(buffer, which, g)
            for i in range(group):
                for start in range(0, part_dev, LANES):
                    k = g * group + i
                    rows = [buffer[k, c : c + 1, start : start + LANES] for c in range(7)]
                    total = add_pairs(targets, rows, total)
            return total

        return lax.fori_loop(1, chips // group, some, some(0, total))

    blocks = LANES // width
    block = lax.broadcasted_iota(jnp.int32, (2, LANES), 1) // width
    first_block = [lax.rem(chip - i + 4 * chips, group) for i in range(group)]
    masks = [[block == lax.rem(q + first_block[i], blocks) for i in range(group)] for q in range(4)]

    def extra_arrival(first, count, half, g):
        others = extra.at[pl.ds(first, count)]
        return pltpu.make_async_remote_copy(
            src_ref=others, dst_ref=others,
            send_sem=bulk_send.at[2], recv_sem=bulk_recv.at[2 + half, g],
            device_id=partner, device_id_type=MESH,
        )

    def over_extra(targets, total):
        groups = chips // group

        def some(g, total):
            if isinstance(g, int):
                if group > 1:
                    extra_arrival(1, group - 1, 0, g).wait_recv()
            else:
                extra_arrival(g * group, group, 0, g).wait_recv()
            extra_arrival(chips + g * group, group, 1, g).wait_recv()
            slots = [extra[g * group + i] + extra[chips + g * group + i] for i in range(group)]
            rows = [None] * 8
            for q in range(4):
                both = jnp.where(masks[q][0], slots[0], 0.0)
                for i in range(1, group):
                    both = jnp.where(masks[q][i], slots[i], both)
                if q > 0:
                    both = pltpu.roll(both, LANES - q * width, 1)
                rows[q], rows[q + 4] = both[0:1], both[1:2]
            return add_pairs(targets, rows, total)

        return some(0, lax.fori_loop(1, groups, lambda i, t: some(groups - i, t), total))

    def columns_of(total):
        return [jnp.sum(part, axis=1, keepdims=True) for part in total]

    def reduced(total):
        return packed(columns_of(total))

    picker_one = picker_of(place_one, list_one)
    tgt1[0] = packed(
        [picked(picker_one, pred_pos[c : c + 1]) for c in range(3)]
        + [picked(picker_one, pred_vel[c : c + 1]) for c in range(3)]
    )
    late_pos, late_vel = predict(pos, vel, acc, jerk, 2 * STEP_BASE)
    src2[0, 0:3, :] = late_pos
    src2[0, 3:6, :] = late_vel
    src2[0, 6:7, :] = jnp.where(hit_one, 0.0, mass)
    src2[0, 7:8, :] = jnp.zeros_like(mass)
    picker_two = picker_of(place_two, list_two)
    window = lane == sub_row + lax.rem(chip, group) * width

    def in_slots(column):
        return jnp.sum(jnp.where(window, column, 0.0), axis=0, keepdims=True)

    slot_state = [
        [in_slots(picked(picker_one, rows[c : c + 1])) for c in range(3)]
        for rows in (pos, vel, acc, jerk)
    ]
    slot_mass = in_slots(picked(picker_one, mass))
    pl.semaphore_wait(barrier, 2 * chips - 1)
    to_pair_one = pair_copy(tgt1, 0)
    to_pair_one.start()
    send_bulk(src1, 0)
    send_bulk(src2, 1)
    to_pair_one.wait_recv()
    targets = targets_of(tgt1[0] + tgt1[1])
    partial = columns_of(over_bulk(targets, src1, zeros(), 0))
    part1[0] = packed(partial)
    sums_one = pair_copy(part1, 1)
    sums_one.start()

    rows = spread_columns(window, partial)
    moved = [None] * 8
    for c in range(3):
        state = correct(
            slot_state[0][c], slot_state[1][c], slot_state[2][c], slot_state[3][c],
            rows[c], rows[c + 3], STEP_BASE, True,
        )
        moved[c], moved[c + 3] = predict(*state, STEP_BASE)
    moved[6], moved[7] = slot_mass, jnp.zeros_like(slot_mass)
    for r in range(2):
        line = moved[4 * r]
        for q in range(1, 4):
            line = line + pltpu.roll(jnp.broadcast_to(moved[4 * r + q], (8, LANES)), q * width, 1)[0:1]
        extra[0, r : r + 1, :] = line
    send_extra()

    sums_one.wait_recv()
    force_one = part1[0] + part1[1]
    rows = spread(picker_one, force_one)
    new_acc, new_jerk = jnp.concatenate(rows[0:3], axis=0), jnp.concatenate(rows[3:6], axis=0)
    pos, vel, acc, jerk = correct(pos, vel, acc, jerk, new_acc, new_jerk, stride, hit_one)

    elapsed = jnp.where(hit_one, STEP_BASE, 2 * STEP_BASE)
    pred_pos, pred_vel = predict(pos, vel, acc, jerk, elapsed)
    tgt2[0] = packed(
        [picked(picker_two, pred_pos[c : c + 1]) for c in range(3)]
        + [picked(picker_two, pred_vel[c : c + 1]) for c in range(3)]
    )
    to_pair_two = pair_copy(tgt2, 2)
    to_pair_two.start()
    for c, row in enumerate(spread(place_one, force_one)):
        fresh_o[c, 0:1, :] = row[:, 0:act]
    own_targets = targets_of(tgt2[0])
    own_total = over_bulk(own_targets, src2, zeros(), 1)
    to_pair_two.wait_recv()
    part2[0] = reduced(over_bulk(targets_of(tgt2[1]), src2, zeros()))
    sums_two = pair_copy(part2, 3)
    sums_two.start()
    own = reduced(over_extra(own_targets, own_total))
    sums_two.wait_recv()
    force_two = own + part2[1]
    rows = spread(picker_two, force_two)
    new_acc, new_jerk = jnp.concatenate(rows[0:3], axis=0), jnp.concatenate(rows[3:6], axis=0)
    pos, vel, acc, jerk = correct(pos, vel, acc, jerk, new_acc, new_jerk, stride, hit_two)
    pos_o[...] = pos
    vel_o[...] = vel
    acc_o[...] = acc
    jerk_o[...] = jerk
    for c, row in enumerate(spread(place_two, force_two)):
        fresh_o[c, 1:2, :] = row[:, 0:act]

    extra_arrival(1, 2 * chips - 1, 0, 0).wait_send()
    for which, buffer in enumerate((src1, src2)):
        arrival(buffer, which, 1, chips - 1, 0).wait_send()
    for copy in (to_pair_one, sums_one, to_pair_two, sums_two):
        copy.wait_send()


def write_out(*refs):
    sems = refs[10]
    copies = [pltpu.make_async_copy(refs[i], refs[5 + i], sems.at[i]) for i in range(5)]
    for copy in copies:
        copy.start()
    for copy in copies:
        copy.wait()


def body(n_blk, n_grp, positions, velocities, accelerations, jerks, mass_weight, levels, active, counts):
    part_dev, act = positions.shape[1], active.shape[1]
    chips = n_blk * n_grp // 2
    state = pltpu.VMEM((3, part_dev), jnp.float32)
    vmem = pltpu.VMEM
    results = pl.pallas_call(
        functools.partial(kernel, n_blk, n_grp, act),
        out_shape=(state, state, state, state, pltpu.VMEM((6, 2, act), jnp.float32)),
        in_specs=[pl.BlockSpec(memory_space=pltpu.HBM)] * 8,
        out_specs=[pl.BlockSpec(memory_space=vmem)] * 5,
        scratch_shapes=[
            vmem((3, part_dev), jnp.float32),
            vmem((3, part_dev), jnp.float32),
            vmem((3, part_dev), jnp.float32),
            vmem((3, part_dev), jnp.float32),
            vmem((1, part_dev), jnp.float32),
            vmem((1, part_dev), jnp.int32),
            vmem((2, act), jnp.int32),
            vmem((1, 2), jnp.int32),
            vmem((chips, 8, part_dev), jnp.float32),
            vmem((chips, 8, part_dev), jnp.float32),
            vmem((2 * chips, 2, LANES), jnp.float32),
            vmem((2, act, LANES), jnp.float32),
            vmem((2, act, LANES), jnp.float32),
            vmem((2, act, LANES), jnp.float32),
            vmem((2, act, LANES), jnp.float32),
            pltpu.SemaphoreType.DMA((8,)),
            pltpu.SemaphoreType.DMA((3,)),
            pltpu.SemaphoreType.DMA((4, chips)),
            pltpu.SemaphoreType.DMA((4,)),
            pltpu.SemaphoreType.DMA((4,)),
        ],
        compiler_params=pltpu.CompilerParams(
            collective_id=0, has_side_effects=True, vmem_limit_bytes=32 * 1024 * 1024
        ),
    )(*[pltpu.with_memory_space_constraint(value, pltpu.HBM) for value in (
        positions, velocities, accelerations, jerks,
        mass_weight.reshape(1, part_dev), levels.reshape(1, part_dev), active, counts.reshape(1, 2),
    )])
    written = pl.pallas_call(
        write_out,
        out_shape=[jax.ShapeDtypeStruct(r.shape, r.dtype) for r in results],
        in_specs=[pl.BlockSpec(memory_space=vmem)] * 5,
        out_specs=[pl.BlockSpec(memory_space=pltpu.HBM)] * 5,
        scratch_shapes=[pltpu.SemaphoreType.DMA((5,))],
        compiler_params=pltpu.CompilerParams(vmem_limit_bytes=1024 * 1024),
    )(*[pltpu.with_memory_space_constraint(value, vmem) for value in results])
    return (*written[0:4], written[4].transpose(1, 0, 2))


def solution(mesh):
    spread_over = ("blk", "grp")
    in_specs = (
        P(None, spread_over),
        P(None, spread_over),
        P(None, spread_over),
        P(None, spread_over),
        P(spread_over),
        P(spread_over),
        P(None, spread_over),
        P(None, spread_over),
    )
    out_specs = (
        P(None, spread_over),
        P(None, spread_over),
        P(None, spread_over),
        P(None, spread_over),
        P(None, None, spread_over),
    )
    inner = functools.partial(body, mesh.shape["blk"], mesh.shape["grp"])
    return jax.shard_map(inner, mesh=mesh, in_specs=in_specs, out_specs=out_specs, check_vma=False)
```

```python
import functools
import math

import jax
import jax.numpy as jnp
from jax import lax
from jax.experimental import pallas as pl
from jax.experimental.pallas import tpu as pltpu
from jax.sharding import PartitionSpec as P

STEP_BASE = 0.125
SOFTEN = 0.01
LANES = 128
MESH = pl.DeviceIdType.MESH


def predict(pos, vel, acc, jerk, elapsed):
    pred_pos = pos + elapsed * (vel + elapsed * (acc * 0.5 + elapsed * jerk / 6.0))
    pred_vel = vel + elapsed * (acc + elapsed * jerk * 0.5)
    return (pred_pos, pred_vel)


def correct(pos, vel, acc, jerk, new_acc, new_jerk, stride, hit):
    half = 0.5 * stride
    square = stride * stride / 12.0
    vel_new = vel + half * (acc + new_acc) + square * (jerk - new_jerk)
    pos_new = pos + half * (vel + vel_new) + square * (acc - new_acc)
    return (
        jnp.where(hit, pos_new, pos),
        jnp.where(hit, vel_new, vel),
        jnp.where(hit, new_acc, acc),
        jnp.where(hit, new_jerk, jerk),
    )


def add_pairs(target, source, total):
    dpos = [source[c] - target[c] for c in range(3)]
    dvel = [source[c + 3] - target[c + 3] for c in range(3)]
    dist = dpos[0] * dpos[0] + dpos[1] * dpos[1] + dpos[2] * dpos[2] + SOFTEN
    inverse = lax.rsqrt(dist)
    square = inverse * inverse
    weight = source[6] * (inverse * square)
    radial = (3.0 * square) * (dpos[0] * dvel[0] + dpos[1] * dvel[1] + dpos[2] * dvel[2])
    accel = [total[c] + weight * dpos[c] for c in range(3)]
    jerk = [total[c + 3] + weight * (dvel[c] - radial * dpos[c]) for c in range(3)]
    return tuple(accel + jerk)


def kernel(
    n_blk, n_grp, act,
    pos_h, vel_h, acc_h, jerk_h, mass_h, lev_h, lists_h, counts_h,
    pos_o, vel_o, acc_o, jerk_o, fresh_o,
    pos_v, vel_v, acc_v, jerk_v, mass_v, lev_v, lists_v, counts_v,
    src1, src2, extra, tgt1, tgt2, part1, part2,
    load_sem, bulk_send, bulk_recv, pair_send, pair_recv,
):
    blk, grp = lax.axis_index("blk"), lax.axis_index("grp")
    per_blk = n_grp // 2
    chips = n_blk * per_blk
    core = lax.rem(grp, 2)
    chip = blk * per_blk + grp // 2
    partner = (blk, grp + 1 - 2 * core)
    part_dev = pos_h.shape[1]
    total_part = part_dev * n_blk * n_grp
    width = 1 << (act - 1).bit_length()
    group = math.gcd(LANES // width, chips)

    def device_at(there, which_core):
        return (there // per_blk, 2 * lax.rem(there, per_blk) + which_core)

    def far_first(visit):
        def turn(j, carry):
            step = ((j + 1) // 2) * (1 - 2 * lax.rem(j, 2))
            there = lax.rem(3 * chips - 1 + step - chip, chips)
            visit(there, lax.rem(there - chip + chips, chips))
            return carry

        lax.fori_loop(0, chips, turn, 0)

    loads = [
        pltpu.make_async_copy(h, v, load_sem.at[i])
        for i, (h, v) in enumerate(
            [(pos_h, pos_v), (vel_h, vel_v), (acc_h, acc_v), (jerk_h, jerk_v),
             (mass_h, mass_v), (lev_h, lev_v), (lists_h, lists_v), (counts_h, counts_v)]
        )
    ]

    barrier = pltpu.get_barrier_semaphore()

    def greet(there, k):
        def signal(which_core):
            pl.semaphore_signal(barrier, inc=1, device_id=device_at(there, which_core), device_id_type=MESH)

        pl.when(k != 0)(lambda: signal(core))
        signal(1 - core)

    far_first(greet)
    for load in loads:
        load.start()

    def send_bulk(buffer, which):
        def send(there, k):
            @pl.when(k != 0)
            def _():
                pltpu.make_async_remote_copy(
                    src_ref=buffer.at[0], dst_ref=buffer.at[k],
                    send_sem=bulk_send.at[which], recv_sem=bulk_recv.at[which, k // group],
                    device_id=device_at(there, core), device_id_type=MESH,
                ).start()

        far_first(send)

    def send_extra():
        def send(there, k):
            def copy(half, which_core):
                pltpu.make_async_remote_copy(
                    src_ref=extra.at[0], dst_ref=extra.at[half * chips + k],
                    send_sem=bulk_send.at[2], recv_sem=bulk_recv.at[2 + half, k // group],
                    device_id=device_at(there, which_core), device_id_type=MESH,
                ).start()

            pl.when(k != 0)(lambda: copy(0, core))
            copy(1, 1 - core)

        far_first(send)

    def arrival(buffer, which, first, count, sems):
        others = buffer.at[pl.ds(first, count)]
        return pltpu.make_async_remote_copy(
            src_ref=others, dst_ref=others,
            send_sem=bulk_send.at[which], recv_sem=bulk_recv.at[which, sems],
            device_id=partner, device_id_type=MESH,
        )

    def await_group(buffer, which, g):
        if isinstance(g, int) and g == 0:
            if group > 1:
                arrival(buffer, which, 1, group - 1, 0).wait_recv()
        else:
            arrival(buffer, which, g * group, group, g).wait_recv()

    def pair_copy(buffer, which):
        return pltpu.make_async_remote_copy(
            src_ref=buffer.at[0], dst_ref=buffer.at[1],
            send_sem=pair_send.at[which], recv_sem=pair_recv.at[which],
            device_id=partner, device_id_type=MESH,
        )

    for load in loads:
        load.wait()
    pos, vel, acc, jerk = pos_v[...], vel_v[...], acc_v[...], jerk_v[...]
    mass = mass_v[...] / total_part
    levels = lev_v[...]
    stride = STEP_BASE * jnp.left_shift(jnp.ones_like(levels), levels).astype(jnp.float32)
    hit_one, hit_two = levels == 0, levels <= 1
    pred_pos, pred_vel = predict(pos, vel, acc, jerk, STEP_BASE)
    src1[0, 0:3, :] = pred_pos
    src1[0, 3:6, :] = pred_vel
    src1[0, 6:7, :] = jnp.where(hit_one, -mass, mass)

    sub_row = lax.broadcasted_iota(jnp.int32, (act, LANES), 0)
    lane = lax.broadcasted_iota(jnp.int32, (act, LANES), 1)
    particle = lax.broadcasted_iota(jnp.int32, (act, part_dev), 1)
    count_one = jnp.broadcast_to(counts_v[0:1, 0:1], (act, LANES))
    count_two = jnp.broadcast_to(counts_v[0:1, 1:2], (act, LANES))
    list_one = jnp.concatenate([lists_v[0:1, :], jnp.zeros((1, LANES - act), jnp.int32)], axis=1)
    list_two = jnp.concatenate([lists_v[1:2, :], jnp.zeros((1, LANES - act), jnp.int32)], axis=1)
    shift = core * (act - count_one)
    place_one = (lane == sub_row - shift) & (lane < count_one)
    place_two = (lane == sub_row) & (lane < count_two)

    def picker_of(place, row):
        value = jnp.where(place, (row + 1).astype(jnp.float32), 0.0)
        column = jnp.sum(value, axis=1, keepdims=True) - 1.0
        return particle.astype(jnp.float32) == column

    def picked(picker, rows):
        return jnp.sum(jnp.where(picker, rows, 0.0), axis=1, keepdims=True)

    def packed(columns):
        tile = jnp.zeros((act, LANES), jnp.float32)
        for c, column in enumerate(columns):
            tile = jnp.where(lane == c, column, tile)
        return tile

    def spread_columns(mask, columns):
        return [jnp.sum(jnp.where(mask, column, 0.0), axis=0, keepdims=True) for column in columns]

    def spread(mask, tile):
        return spread_columns(mask, [tile[:, c : c + 1] for c in range(6)])

    def targets_of(tile):
        return [jnp.broadcast_to(tile[:, c : c + 1], (act, LANES)) for c in range(6)]

    def zeros():
        return tuple(jnp.zeros((act, LANES), jnp.float32) for _ in range(6))

    def over_bulk(targets, buffer, total, which=None, after_first=None):
        def some(g, total):
            if which is not None:
                await_group(buffer, which, g)
            for i in range(group):
                for start in range(0, part_dev, LANES):
                    k = g * group + i
                    rows = [buffer[k, c : c + 1, start : start + LANES] for c in range(6)]
                    signed = src1[k, 6:7, start : start + LANES]
                    rows.append(jnp.abs(signed) if buffer is src1 else jnp.maximum(signed, 0.0))
                    total = add_pairs(targets, rows, total)
            return total

        total = some(0, total)
        if after_first is not None:
            after_first()
        return lax.fori_loop(1, chips // group, some, total)

    blocks = LANES // width
    block = lax.broadcasted_iota(jnp.int32, (2, LANES), 1) // width
    first_block = [lax.rem(chip - i + 4 * chips, group) for i in range(group)]
    masks = [[block == lax.rem(q + first_block[i], blocks) for i in range(group)] for q in range(4)]

    def extra_arrival(first, count, half, g):
        others = extra.at[pl.ds(first, count)]
        return pltpu.make_async_remote_copy(
            src_ref=others, dst_ref=others,
            send_sem=bulk_send.at[2], recv_sem=bulk_recv.at[2 + half, g],
            device_id=partner, device_id_type=MESH,
        )

    def over_extra(targets, total):
        groups = chips // group

        def some(g, total):
            if isinstance(g, int):
                if group > 1:
                    extra_arrival(1, group - 1, 0, g).wait_recv()
            else:
                extra_arrival(g * group, group, 0, g).wait_recv()
            extra_arrival(chips + g * group, group, 1, g).wait_recv()
            slots = [extra[g * group + i] + extra[chips + g * group + i] for i in range(group)]
            rows = [None] * 8
            for q in range(4):
                both = jnp.where(masks[q][0], slots[0], 0.0)
                for i in range(1, group):
                    both = jnp.where(masks[q][i], slots[i], both)
                if q > 0:
                    both = pltpu.roll(both, LANES - q * width, 1)
                rows[q], rows[q + 4] = both[0:1], both[1:2]
            return add_pairs(targets, rows, total)

        return some(0, lax.fori_loop(1, groups, lambda i, t: some(groups - i, t), total))

    def columns_of(total):
        return [jnp.sum(part, axis=1, keepdims=True) for part in total]

    def reduced(total):
        return packed(columns_of(total))

    picker_one = picker_of(place_one, list_one)
    tgt1[0] = packed(
        [picked(picker_one, pred_pos[c : c + 1]) for c in range(3)]
        + [picked(picker_one, pred_vel[c : c + 1]) for c in range(3)]
    )
    late_pos, late_vel = predict(pos, vel, acc, jerk, 2 * STEP_BASE)
    src2[0, 0:3, :] = late_pos
    src2[0, 3:6, :] = late_vel
    picker_two = picker_of(place_two, list_two)
    window = lane == sub_row + lax.rem(chip, group) * width

    def in_slots(column):
        return jnp.sum(jnp.where(window, column, 0.0), axis=0, keepdims=True)

    slot_state = [
        [in_slots(picked(picker_one, rows[c : c + 1])) for c in range(3)]
        for rows in (pos, vel, acc, jerk)
    ]
    slot_mass = in_slots(picked(picker_one, mass))
    pl.semaphore_wait(barrier, 2 * chips - 1)
    to_pair_one = pair_copy(tgt1, 0)
    to_pair_one.start()
    send_bulk(src1, 0)
    to_pair_one.wait_recv()
    targets = targets_of(tgt1[0] + tgt1[1])
    partial = columns_of(over_bulk(targets, src1, zeros(), 0, lambda: send_bulk(src2, 1)))
    part1[0] = packed(partial)
    sums_one = pair_copy(part1, 1)
    sums_one.start()

    rows = spread_columns(window, partial)
    moved = [None] * 8
    for c in range(3):
        state = correct(
            slot_state[0][c], slot_state[1][c], slot_state[2][c], slot_state[3][c],
            rows[c], rows[c + 3], STEP_BASE, True,
        )
        moved[c], moved[c + 3] = predict(*state, STEP_BASE)
    moved[6], moved[7] = slot_mass, jnp.zeros_like(slot_mass)
    for r in range(2):
        line = moved[4 * r]
        for q in range(1, 4):
            line = line + pltpu.roll(jnp.broadcast_to(moved[4 * r + q], (8, LANES)), q * width, 1)[0:1]
        extra[0, r : r + 1, :] = line
    send_extra()

    sums_one.wait_recv()
    force_one = part1[0] + part1[1]
    rows = spread(picker_one, force_one)
    new_acc, new_jerk = jnp.concatenate(rows[0:3], axis=0), jnp.concatenate(rows[3:6], axis=0)
    pos, vel, acc, jerk = correct(pos, vel, acc, jerk, new_acc, new_jerk, stride, hit_one)

    elapsed = jnp.where(hit_one, STEP_BASE, 2 * STEP_BASE)
    pred_pos, pred_vel = predict(pos, vel, acc, jerk, elapsed)
    tgt2[0] = packed(
        [picked(picker_two, pred_pos[c : c + 1]) for c in range(3)]
        + [picked(picker_two, pred_vel[c : c + 1]) for c in range(3)]
    )
    to_pair_two = pair_copy(tgt2, 2)
    to_pair_two.start()
    for c, row in enumerate(spread(place_one, force_one)):
        fresh_o[c, 0:1, :] = row[:, 0:act]
    own_targets = targets_of(tgt2[0])
    own_total = over_bulk(own_targets, src2, zeros(), 1)
    to_pair_two.wait_recv()
    part2[0] = reduced(over_bulk(targets_of(tgt2[1]), src2, zeros()))
    sums_two = pair_copy(part2, 3)
    sums_two.start()
    own = reduced(over_extra(own_targets, own_total))
    sums_two.wait_recv()
    force_two = own + part2[1]
    rows = spread(picker_two, force_two)
    new_acc, new_jerk = jnp.concatenate(rows[0:3], axis=0), jnp.concatenate(rows[3:6], axis=0)
    pos, vel, acc, jerk = correct(pos, vel, acc, jerk, new_acc, new_jerk, stride, hit_two)
    pos_o[...] = pos
    vel_o[...] = vel
    acc_o[...] = acc
    jerk_o[...] = jerk
    for c, row in enumerate(spread(place_two, force_two)):
        fresh_o[c, 1:2, :] = row[:, 0:act]

    extra_arrival(1, 2 * chips - 1, 0, 0).wait_send()
    for which, buffer in enumerate((src1, src2)):
        arrival(buffer, which, 1, chips - 1, 0).wait_send()
    for copy in (to_pair_one, sums_one, to_pair_two, sums_two):
        copy.wait_send()


def write_out(*refs):
    sems = refs[10]
    copies = [pltpu.make_async_copy(refs[i], refs[5 + i], sems.at[i]) for i in range(5)]
    for copy in copies:
        copy.start()
    for copy in copies:
        copy.wait()


def body(n_blk, n_grp, positions, velocities, accelerations, jerks, mass_weight, levels, active, counts):
    part_dev, act = positions.shape[1], active.shape[1]
    chips = n_blk * n_grp // 2
    state = pltpu.VMEM((3, part_dev), jnp.float32)
    vmem = pltpu.VMEM
    results = pl.pallas_call(
        functools.partial(kernel, n_blk, n_grp, act),
        out_shape=(state, state, state, state, pltpu.VMEM((6, 2, act), jnp.float32)),
        in_specs=[pl.BlockSpec(memory_space=pltpu.HBM)] * 8,
        out_specs=[pl.BlockSpec(memory_space=vmem)] * 5,
        scratch_shapes=[
            vmem((3, part_dev), jnp.float32),
            vmem((3, part_dev), jnp.float32),
            vmem((3, part_dev), jnp.float32),
            vmem((3, part_dev), jnp.float32),
            vmem((1, part_dev), jnp.float32),
            vmem((1, part_dev), jnp.int32),
            vmem((2, act), jnp.int32),
            vmem((1, 2), jnp.int32),
            vmem((chips, 7, part_dev), jnp.float32),
            vmem((chips, 6, part_dev), jnp.float32),
            vmem((2 * chips, 2, LANES), jnp.float32),
            vmem((2, act, LANES), jnp.float32),
            vmem((2, act, LANES), jnp.float32),
            vmem((2, act, LANES), jnp.float32),
            vmem((2, act, LANES), jnp.float32),
            pltpu.SemaphoreType.DMA((8,)),
            pltpu.SemaphoreType.DMA((3,)),
            pltpu.SemaphoreType.DMA((4, chips)),
            pltpu.SemaphoreType.DMA((4,)),
            pltpu.SemaphoreType.DMA((4,)),
        ],
        compiler_params=pltpu.CompilerParams(
            collective_id=0, has_side_effects=True, vmem_limit_bytes=32 * 1024 * 1024
        ),
    )(*[pltpu.with_memory_space_constraint(value, pltpu.HBM) for value in (
        positions, velocities, accelerations, jerks,
        mass_weight.reshape(1, part_dev), levels.reshape(1, part_dev), active, counts.reshape(1, 2),
    )])
    written = pl.pallas_call(
        write_out,
        out_shape=[jax.ShapeDtypeStruct(r.shape, r.dtype) for r in results],
        in_specs=[pl.BlockSpec(memory_space=vmem)] * 5,
        out_specs=[pl.BlockSpec(memory_space=pltpu.HBM)] * 5,
        scratch_shapes=[pltpu.SemaphoreType.DMA((5,))],
        compiler_params=pltpu.CompilerParams(vmem_limit_bytes=1024 * 1024),
    )(*[pltpu.with_memory_space_constraint(value, vmem) for value in results])
    return (*written[0:4], written[4].transpose(1, 0, 2))


def solution(mesh):
    spread_over = ("blk", "grp")
    in_specs = (
        P(None, spread_over),
        P(None, spread_over),
        P(None, spread_over),
        P(None, spread_over),
        P(spread_over),
        P(spread_over),
        P(None, spread_over),
        P(None, spread_over),
    )
    out_specs = (
        P(None, spread_over),
        P(None, spread_over),
        P(None, spread_over),
        P(None, spread_over),
        P(None, None, spread_over),
    )
    inner = functools.partial(body, mesh.shape["blk"], mesh.shape["grp"])
    return jax.shard_map(inner, mesh=mesh, in_specs=in_specs, out_specs=out_specs, check_vma=False)
```

```python
import functools
import math

import jax
import jax.numpy as jnp
from jax import lax
from jax.experimental import pallas as pl
from jax.experimental.pallas import tpu as pltpu
from jax.sharding import PartitionSpec as P

STEP_BASE = 0.125
SOFTEN = 0.01
LANES = 128
MESH = pl.DeviceIdType.MESH


def predict(pos, vel, acc, jerk, elapsed):
    pred_pos = pos + elapsed * (vel + elapsed * (acc * 0.5 + elapsed * jerk / 6.0))
    pred_vel = vel + elapsed * (acc + elapsed * jerk * 0.5)
    return (pred_pos, pred_vel)


def correct(pos, vel, acc, jerk, new_acc, new_jerk, stride, hit):
    half = 0.5 * stride
    square = stride * stride / 12.0
    vel_new = vel + half * (acc + new_acc) + square * (jerk - new_jerk)
    pos_new = pos + half * (vel + vel_new) + square * (acc - new_acc)
    return (
        jnp.where(hit, pos_new, pos),
        jnp.where(hit, vel_new, vel),
        jnp.where(hit, new_acc, acc),
        jnp.where(hit, new_jerk, jerk),
    )


def add_pairs(target, source, total):
    dpos = [source[c] - target[c] for c in range(3)]
    dvel = [source[c + 3] - target[c + 3] for c in range(3)]
    dist = dpos[0] * dpos[0] + dpos[1] * dpos[1] + dpos[2] * dpos[2] + SOFTEN
    inverse = lax.rsqrt(dist)
    square = inverse * inverse
    weight = source[6] * (inverse * square)
    radial = (3.0 * square) * (dpos[0] * dvel[0] + dpos[1] * dvel[1] + dpos[2] * dvel[2])
    accel = [total[c] + weight * dpos[c] for c in range(3)]
    jerk = [total[c + 3] + weight * (dvel[c] - radial * dpos[c]) for c in range(3)]
    return tuple(accel + jerk)


def kernel(
    n_blk, n_grp, act,
    pos_h, vel_h, acc_h, jerk_h, mass_h, lev_h, lists_h, counts_h,
    pos_o, vel_o, acc_o, jerk_o, fresh_o,
    pos_v, vel_v, acc_v, jerk_v, mass_v, lev_v, lists_v, counts_v,
    src1, src2, extra, tgt1, tgt2, part1, part2,
    load_sem, bulk_send, bulk_recv, pair_send, pair_recv,
):
    blk, grp = lax.axis_index("blk"), lax.axis_index("grp")
    per_blk = n_grp // 2
    chips = n_blk * per_blk
    core = lax.rem(grp, 2)
    chip = blk * per_blk + grp // 2
    partner = (blk, grp + 1 - 2 * core)
    part_dev = pos_h.shape[1]
    total_part = part_dev * n_blk * n_grp
    width = 1 << (act - 1).bit_length()
    group = math.gcd(LANES // width, chips)

    def device_at(there, which_core):
        return (there // per_blk, 2 * lax.rem(there, per_blk) + which_core)

    def far_first(visit):
        def turn(j, carry):
            step = ((j + 1) // 2) * (1 - 2 * lax.rem(j, 2))
            there = lax.rem(3 * chips - 1 + step - chip, chips)
            visit(there, lax.rem(there - chip + chips, chips))
            return carry

        lax.fori_loop(0, chips, turn, 0)

    loads = [
        pltpu.make_async_copy(h, v, load_sem.at[i])
        for i, (h, v) in enumerate(
            [(pos_h, pos_v), (vel_h, vel_v), (acc_h, acc_v), (jerk_h, jerk_v),
             (mass_h, mass_v), (lev_h, lev_v), (lists_h, lists_v), (counts_h, counts_v)]
        )
    ]

    barrier = pltpu.get_barrier_semaphore()

    def greet(there, k):
        def signal(which_core):
            pl.semaphore_signal(barrier, inc=1, device_id=device_at(there, which_core), device_id_type=MESH)

        pl.when(k != 0)(lambda: signal(core))
        signal(1 - core)

    far_first(greet)
    for load in loads:
        load.start()

    def send_bulk(buffer, which):
        def send(there, k):
            @pl.when(k != 0)
            def _():
                pltpu.make_async_remote_copy(
                    src_ref=buffer.at[0], dst_ref=buffer.at[k],
                    send_sem=bulk_send.at[which], recv_sem=bulk_recv.at[which, k // group],
                    device_id=device_at(there, core), device_id_type=MESH,
                ).start()

        far_first(send)

    def send_extra():
        def send(there, k):
            def copy(half, which_core):
                pltpu.make_async_remote_copy(
                    src_ref=extra.at[0], dst_ref=extra.at[half * chips + k],
                    send_sem=bulk_send.at[2], recv_sem=bulk_recv.at[2 + half, k // group],
                    device_id=device_at(there, which_core), device_id_type=MESH,
                ).start()

            pl.when(k != 0)(lambda: copy(0, core))
            copy(1, 1 - core)

        far_first(send)

    def arrival(buffer, which, first, count, sems):
        others = buffer.at[pl.ds(first, count)]
        return pltpu.make_async_remote_copy(
            src_ref=others, dst_ref=others,
            send_sem=bulk_send.at[which], recv_sem=bulk_recv.at[which, sems],
            device_id=partner, device_id_type=MESH,
        )

    def await_group(buffer, which, g):
        if isinstance(g, int) and g == 0:
            if group > 1:
                arrival(buffer, which, 1, group - 1, 0).wait_recv()
        else:
            arrival(buffer, which, g * group, group, g).wait_recv()

    def pair_copy(buffer, which):
        return pltpu.make_async_remote_copy(
            src_ref=buffer.at[0], dst_ref=buffer.at[1],
            send_sem=pair_send.at[which], recv_sem=pair_recv.at[which],
            device_id=partner, device_id_type=MESH,
        )

    for load in loads:
        load.wait()
    pos, vel, acc, jerk = pos_v[...], vel_v[...], acc_v[...], jerk_v[...]
    mass = mass_v[...] / total_part
    levels = lev_v[...]
    stride = STEP_BASE * jnp.left_shift(jnp.ones_like(levels), levels).astype(jnp.float32)
    hit_one, hit_two = levels == 0, levels <= 1
    pred_pos, pred_vel = predict(pos, vel, acc, jerk, STEP_BASE)
    src1[0, 0:3, :] = pred_pos
    src1[0, 3:6, :] = pred_vel
    src1[0, 6:7, :] = jnp.where(hit_one, -mass, mass)

    sub_row = lax.broadcasted_iota(jnp.int32, (act, LANES), 0)
    lane = lax.broadcasted_iota(jnp.int32, (act, LANES), 1)
    particle = lax.broadcasted_iota(jnp.int32, (act, part_dev), 1)
    count_one = jnp.broadcast_to(counts_v[0:1, 0:1], (act, LANES))
    count_two = jnp.broadcast_to(counts_v[0:1, 1:2], (act, LANES))
    list_one = jnp.concatenate([lists_v[0:1, :], jnp.zeros((1, LANES - act), jnp.int32)], axis=1)
    list_two = jnp.concatenate([lists_v[1:2, :], jnp.zeros((1, LANES - act), jnp.int32)], axis=1)
    shift = core * (act - count_one)
    place_one = (lane == sub_row - shift) & (lane < count_one)
    place_two = (lane == sub_row) & (lane < count_two)

    def picker_of(place, row):
        value = jnp.where(place, (row + 1).astype(jnp.float32), 0.0)
        column = jnp.sum(value, axis=1, keepdims=True) - 1.0
        return particle.astype(jnp.float32) == column

    def picked(picker, rows):
        return jnp.sum(jnp.where(picker, rows, 0.0), axis=1, keepdims=True)

    def packed(columns):
        tile = jnp.zeros((act, LANES), jnp.float32)
        for c, column in enumerate(columns):
            tile = jnp.where(lane == c, column, tile)
        return tile

    def spread_columns(mask, columns):
        return [jnp.sum(jnp.where(mask, column, 0.0), axis=0, keepdims=True) for column in columns]

    def spread(mask, tile):
        return spread_columns(mask, [tile[:, c : c + 1] for c in range(6)])

    def targets_of(tile):
        return [jnp.broadcast_to(tile[:, c : c + 1], (act, LANES)) for c in range(6)]

    def zeros():
        return tuple(jnp.zeros((act, LANES), jnp.float32) for _ in range(6))

    def over_bulk(targets, buffer, total, which=None):
        def some(g, total):
            if which is not None:
                await_group(buffer, which, g)
            for i in range(group):
                for start in range(0, part_dev, LANES):
                    k = g * group + i
                    rows = [buffer[k, c : c + 1, start : start + LANES] for c in range(6)]
                    signed = src1[k, 6:7, start : start + LANES]
                    rows.append(jnp.abs(signed) if buffer is src1 else jnp.maximum(signed, 0.0))
                    total = add_pairs(targets, rows, total)
            return total

        return lax.fori_loop(1, chips // group, some, some(0, total))

    blocks = LANES // width
    block = lax.broadcasted_iota(jnp.int32, (2, LANES), 1) // width
    first_block = [lax.rem(chip - i + 4 * chips, group) for i in range(group)]
    masks = [[block == lax.rem(q + first_block[i], blocks) for i in range(group)] for q in range(4)]

    def extra_arrival(first, count, half, g):
        others = extra.at[pl.ds(first, count)]
        return pltpu.make_async_remote_copy(
            src_ref=others, dst_ref=others,
            send_sem=bulk_send.at[2], recv_sem=bulk_recv.at[2 + half, g],
            device_id=partner, device_id_type=MESH,
        )

    def over_extra(targets, total):
        groups = chips // group

        def some(g, total):
            if isinstance(g, int):
                if group > 1:
                    extra_arrival(1, group - 1, 0, g).wait_recv()
            else:
                extra_arrival(g * group, group, 0, g).wait_recv()
            extra_arrival(chips + g * group, group, 1, g).wait_recv()
            slots = [extra[g * group + i] + extra[chips + g * group + i] for i in range(group)]
            rows = [None] * 8
            for q in range(4):
                both = jnp.where(masks[q][0], slots[0], 0.0)
                for i in range(1, group):
                    both = jnp.where(masks[q][i], slots[i], both)
                if q > 0:
                    both = pltpu.roll(both, LANES - q * width, 1)
                rows[q], rows[q + 4] = both[0:1], both[1:2]
            return add_pairs(targets, rows, total)

        return some(0, lax.fori_loop(1, groups, lambda i, t: some(groups - i, t), total))

    def columns_of(total):
        return [jnp.sum(part, axis=1, keepdims=True) for part in total]

    def reduced(total):
        return packed(columns_of(total))

    picker_one = picker_of(place_one, list_one)
    tgt1[0] = packed(
        [picked(picker_one, pred_pos[c : c + 1]) for c in range(3)]
        + [picked(picker_one, pred_vel[c : c + 1]) for c in range(3)]
    )
    late_pos, late_vel = predict(pos, vel, acc, jerk, 2 * STEP_BASE)
    src2[0, 0:3, :] = late_pos
    src2[0, 3:6, :] = late_vel
    picker_two = picker_of(place_two, list_two)
    window = lane == sub_row + lax.rem(chip, group) * width

    def in_slots(column):
        return jnp.sum(jnp.where(window, column, 0.0), axis=0, keepdims=True)

    slot_state = [
        [in_slots(picked(picker_one, rows[c : c + 1])) for c in range(3)]
        for rows in (pos, vel, acc, jerk)
    ]
    slot_mass = in_slots(picked(picker_one, mass))
    pl.semaphore_wait(barrier, 2 * chips - 1)
    to_pair_one = pair_copy(tgt1, 0)
    to_pair_one.start()
    send_bulk(src1, 0)
    to_pair_one.wait_recv()
    send_bulk(src2, 1)
    targets = targets_of(tgt1[0] + tgt1[1])
    partial = columns_of(over_bulk(targets, src1, zeros(), 0))
    part1[0] = packed(partial)
    sums_one = pair_copy(part1, 1)
    sums_one.start()

    rows = spread_columns(window, partial)
    moved = [None] * 8
    for c in range(3):
        state = correct(
            slot_state[0][c], slot_state[1][c], slot_state[2][c], slot_state[3][c],
            rows[c], rows[c + 3], STEP_BASE, True,
        )
        moved[c], moved[c + 3] = predict(*state, STEP_BASE)
    moved[6], moved[7] = slot_mass, jnp.zeros_like(slot_mass)
    for r in range(2):
        line = moved[4 * r]
        for q in range(1, 4):
            line = line + pltpu.roll(jnp.broadcast_to(moved[4 * r + q], (8, LANES)), q * width, 1)[0:1]
        extra[0, r : r + 1, :] = line
    send_extra()

    sums_one.wait_recv()
    force_one = part1[0] + part1[1]
    rows = spread(picker_one, force_one)
    new_acc, new_jerk = jnp.concatenate(rows[0:3], axis=0), jnp.concatenate(rows[3:6], axis=0)
    pos, vel, acc, jerk = correct(pos, vel, acc, jerk, new_acc, new_jerk, stride, hit_one)

    elapsed = jnp.where(hit_one, STEP_BASE, 2 * STEP_BASE)
    pred_pos, pred_vel = predict(pos, vel, acc, jerk, elapsed)
    tgt2[0] = packed(
        [picked(picker_two, pred_pos[c : c + 1]) for c in range(3)]
        + [picked(picker_two, pred_vel[c : c + 1]) for c in range(3)]
    )
    to_pair_two = pair_copy(tgt2, 2)
    to_pair_two.start()
    for c, row in enumerate(spread(place_one, force_one)):
        fresh_o[c, 0:1, :] = row[:, 0:act]
    own_targets = targets_of(tgt2[0])
    own_total = over_bulk(own_targets, src2, zeros(), 1)
    to_pair_two.wait_recv()
    part2[0] = reduced(over_bulk(targets_of(tgt2[1]), src2, zeros()))
    sums_two = pair_copy(part2, 3)
    sums_two.start()
    own = reduced(over_extra(own_targets, own_total))
    sums_two.wait_recv()
    force_two = own + part2[1]
    rows = spread(picker_two, force_two)
    new_acc, new_jerk = jnp.concatenate(rows[0:3], axis=0), jnp.concatenate(rows[3:6], axis=0)
    pos, vel, acc, jerk = correct(pos, vel, acc, jerk, new_acc, new_jerk, stride, hit_two)
    pos_o[...] = pos
    vel_o[...] = vel
    acc_o[...] = acc
    jerk_o[...] = jerk
    for c, row in enumerate(spread(place_two, force_two)):
        fresh_o[c, 1:2, :] = row[:, 0:act]

    extra_arrival(1, 2 * chips - 1, 0, 0).wait_send()
    for which, buffer in enumerate((src1, src2)):
        arrival(buffer, which, 1, chips - 1, 0).wait_send()
    for copy in (to_pair_one, sums_one, to_pair_two, sums_two):
        copy.wait_send()


def write_out(*refs):
    sems = refs[10]
    copies = [pltpu.make_async_copy(refs[i], refs[5 + i], sems.at[i]) for i in range(5)]
    for copy in copies:
        copy.start()
    for copy in copies:
        copy.wait()


def body(n_blk, n_grp, positions, velocities, accelerations, jerks, mass_weight, levels, active, counts):
    part_dev, act = positions.shape[1], active.shape[1]
    chips = n_blk * n_grp // 2
    state = pltpu.VMEM((3, part_dev), jnp.float32)
    vmem = pltpu.VMEM
    results = pl.pallas_call(
        functools.partial(kernel, n_blk, n_grp, act),
        out_shape=(state, state, state, state, pltpu.VMEM((6, 2, act), jnp.float32)),
        in_specs=[pl.BlockSpec(memory_space=pltpu.HBM)] * 8,
        out_specs=[pl.BlockSpec(memory_space=vmem)] * 5,
        scratch_shapes=[
            vmem((3, part_dev), jnp.float32),
            vmem((3, part_dev), jnp.float32),
            vmem((3, part_dev), jnp.float32),
            vmem((3, part_dev), jnp.float32),
            vmem((1, part_dev), jnp.float32),
            vmem((1, part_dev), jnp.int32),
            vmem((2, act), jnp.int32),
            vmem((1, 2), jnp.int32),
            vmem((chips, 7, part_dev), jnp.float32),
            vmem((chips, 6, part_dev), jnp.float32),
            vmem((2 * chips, 2, LANES), jnp.float32),
            vmem((2, act, LANES), jnp.float32),
            vmem((2, act, LANES), jnp.float32),
            vmem((2, act, LANES), jnp.float32),
            vmem((2, act, LANES), jnp.float32),
            pltpu.SemaphoreType.DMA((8,)),
            pltpu.SemaphoreType.DMA((3,)),
            pltpu.SemaphoreType.DMA((4, chips)),
            pltpu.SemaphoreType.DMA((4,)),
            pltpu.SemaphoreType.DMA((4,)),
        ],
        compiler_params=pltpu.CompilerParams(
            collective_id=0, has_side_effects=True, vmem_limit_bytes=32 * 1024 * 1024
        ),
    )(*[pltpu.with_memory_space_constraint(value, pltpu.HBM) for value in (
        positions, velocities, accelerations, jerks,
        mass_weight.reshape(1, part_dev), levels.reshape(1, part_dev), active, counts.reshape(1, 2),
    )])
    written = pl.pallas_call(
        write_out,
        out_shape=[jax.ShapeDtypeStruct(r.shape, r.dtype) for r in results],
        in_specs=[pl.BlockSpec(memory_space=vmem)] * 5,
        out_specs=[pl.BlockSpec(memory_space=pltpu.HBM)] * 5,
        scratch_shapes=[pltpu.SemaphoreType.DMA((5,))],
        compiler_params=pltpu.CompilerParams(vmem_limit_bytes=1024 * 1024),
    )(*[pltpu.with_memory_space_constraint(value, vmem) for value in results])
    return (*written[0:4], written[4].transpose(1, 0, 2))


def solution(mesh):
    spread_over = ("blk", "grp")
    in_specs = (
        P(None, spread_over),
        P(None, spread_over),
        P(None, spread_over),
        P(None, spread_over),
        P(spread_over),
        P(spread_over),
        P(None, spread_over),
        P(None, spread_over),
    )
    out_specs = (
        P(None, spread_over),
        P(None, spread_over),
        P(None, spread_over),
        P(None, spread_over),
        P(None, None, spread_over),
    )
    inner = functools.partial(body, mesh.shape["blk"], mesh.shape["grp"])
    return jax.shard_map(inner, mesh=mesh, in_specs=in_specs, out_specs=out_specs, check_vma=False)
```

```python
import functools
import math

import jax
import jax.numpy as jnp
from jax import lax
from jax.experimental import pallas as pl
from jax.experimental.pallas import tpu as pltpu
from jax.sharding import PartitionSpec as P

STEP_BASE = 0.125
SOFTEN = 0.01
LANES = 128
MESH = pl.DeviceIdType.MESH


def predict(pos, vel, acc, jerk, elapsed):
    pred_pos = pos + elapsed * (vel + elapsed * (acc * 0.5 + elapsed * jerk / 6.0))
    pred_vel = vel + elapsed * (acc + elapsed * jerk * 0.5)
    return (pred_pos, pred_vel)


def correct(pos, vel, acc, jerk, new_acc, new_jerk, stride, hit):
    half = 0.5 * stride
    square = stride * stride / 12.0
    vel_new = vel + half * (acc + new_acc) + square * (jerk - new_jerk)
    pos_new = pos + half * (vel + vel_new) + square * (acc - new_acc)
    return (
        jnp.where(hit, pos_new, pos),
        jnp.where(hit, vel_new, vel),
        jnp.where(hit, new_acc, acc),
        jnp.where(hit, new_jerk, jerk),
    )


def add_pairs(target, source, total):
    dpos = [source[c] - target[c] for c in range(3)]
    dvel = [source[c + 3] - target[c + 3] for c in range(3)]
    dist = dpos[0] * dpos[0] + dpos[1] * dpos[1] + dpos[2] * dpos[2] + SOFTEN
    inverse = lax.rsqrt(dist)
    square = inverse * inverse
    weight = source[6] * (inverse * square)
    radial = (3.0 * square) * (dpos[0] * dvel[0] + dpos[1] * dvel[1] + dpos[2] * dvel[2])
    accel = [total[c] + weight * dpos[c] for c in range(3)]
    jerk = [total[c + 3] + weight * (dvel[c] - radial * dpos[c]) for c in range(3)]
    return tuple(accel + jerk)


def kernel(
    n_blk, n_grp, act,
    pos_h, vel_h, acc_h, jerk_h, mass_h, lev_h, lists_h, counts_h,
    pos_o, vel_o, acc_o, jerk_o, fresh_o,
    pos_v, vel_v, acc_v, jerk_v, mass_v, lev_v, lists_v, counts_v,
    src1, src2, extra, tgt1, tgt2, part1, part2,
    load_sem, bulk_send, bulk_recv, pair_send, pair_recv,
):
    blk, grp = lax.axis_index("blk"), lax.axis_index("grp")
    per_blk = n_grp // 2
    chips = n_blk * per_blk
    core = lax.rem(grp, 2)
    chip = blk * per_blk + grp // 2
    partner = (blk, grp + 1 - 2 * core)
    part_dev = pos_h.shape[1]
    total_part = part_dev * n_blk * n_grp
    width = 1 << (act - 1).bit_length()
    group = math.gcd(LANES // width, chips)

    def device_at(there, which_core):
        return (there // per_blk, 2 * lax.rem(there, per_blk) + which_core)

    def far_first(visit):
        def turn(j, carry):
            step = ((j + 1) // 2) * (1 - 2 * lax.rem(j, 2))
            there = lax.rem(3 * chips - 1 + step - chip, chips)
            visit(there, lax.rem(there - chip + chips, chips))
            return carry

        lax.fori_loop(0, chips, turn, 0)

    loads = [
        pltpu.make_async_copy(h, v, load_sem.at[i])
        for i, (h, v) in enumerate(
            [(pos_h, pos_v), (vel_h, vel_v), (acc_h, acc_v), (jerk_h, jerk_v),
             (mass_h, mass_v), (lev_h, lev_v), (lists_h, lists_v), (counts_h, counts_v)]
        )
    ]

    barrier = pltpu.get_barrier_semaphore()

    def greet(there, k):
        def signal(which_core):
            pl.semaphore_signal(barrier, inc=1, device_id=device_at(there, which_core), device_id_type=MESH)

        pl.when(k != 0)(lambda: signal(core))
        signal(1 - core)

    far_first(greet)
    for load in loads:
        load.start()

    def send_bulk(buffer, which):
        def send(there, k):
            @pl.when(k != 0)
            def _():
                pltpu.make_async_remote_copy(
                    src_ref=buffer.at[0], dst_ref=buffer.at[k],
                    send_sem=bulk_send.at[which], recv_sem=bulk_recv.at[which, k // group],
                    device_id=device_at(there, core), device_id_type=MESH,
                ).start()

        far_first(send)

    def send_extra():
        def send(there, k):
            def copy(half, which_core):
                pltpu.make_async_remote_copy(
                    src_ref=extra.at[0], dst_ref=extra.at[half * chips + k],
                    send_sem=bulk_send.at[2], recv_sem=bulk_recv.at[2 + half, k // group],
                    device_id=device_at(there, which_core), device_id_type=MESH,
                ).start()

            pl.when(k != 0)(lambda: copy(0, core))
            copy(1, 1 - core)

        far_first(send)

    def arrival(buffer, which, first, count, sems):
        others = buffer.at[pl.ds(first, count)]
        return pltpu.make_async_remote_copy(
            src_ref=others, dst_ref=others,
            send_sem=bulk_send.at[which], recv_sem=bulk_recv.at[which, sems],
            device_id=partner, device_id_type=MESH,
        )

    def await_group(buffer, which, g):
        if isinstance(g, int) and g == 0:
            if group > 1:
                arrival(buffer, which, 1, group - 1, 0).wait_recv()
        else:
            arrival(buffer, which, g * group, group, g).wait_recv()

    def pair_copy(buffer, which):
        return pltpu.make_async_remote_copy(
            src_ref=buffer.at[0], dst_ref=buffer.at[1],
            send_sem=pair_send.at[which], recv_sem=pair_recv.at[which],
            device_id=partner, device_id_type=MESH,
        )

    for load in loads:
        load.wait()
    pos, vel, acc, jerk = pos_v[...], vel_v[...], acc_v[...], jerk_v[...]
    mass = mass_v[...] / total_part
    levels = lev_v[...]
    stride = STEP_BASE * jnp.left_shift(jnp.ones_like(levels), levels).astype(jnp.float32)
    hit_one, hit_two = levels == 0, levels <= 1
    pred_pos, pred_vel = predict(pos, vel, acc, jerk, STEP_BASE)
    src1[0, 0:3, :] = pred_pos
    src1[0, 3:6, :] = pred_vel
    src1[0, 6:7, :] = jnp.where(hit_one, -mass, mass)

    sub_row = lax.broadcasted_iota(jnp.int32, (act, LANES), 0)
    lane = lax.broadcasted_iota(jnp.int32, (act, LANES), 1)
    particle = lax.broadcasted_iota(jnp.int32, (act, part_dev), 1)
    count_one = jnp.broadcast_to(counts_v[0:1, 0:1], (act, LANES))
    count_two = jnp.broadcast_to(counts_v[0:1, 1:2], (act, LANES))
    list_one = jnp.concatenate([lists_v[0:1, :], jnp.zeros((1, LANES - act), jnp.int32)], axis=1)
    list_two = jnp.concatenate([lists_v[1:2, :], jnp.zeros((1, LANES - act), jnp.int32)], axis=1)
    shift = core * (act - count_one)
    place_one = (lane == sub_row - shift) & (lane < count_one)
    place_two = (lane == sub_row) & (lane < count_two)

    def picker_of(place, row):
        value = jnp.where(place, (row + 1).astype(jnp.float32), 0.0)
        column = jnp.sum(value, axis=1, keepdims=True) - 1.0
        return particle.astype(jnp.float32) == column

    def picked(picker, rows):
        return jnp.sum(jnp.where(picker, rows, 0.0), axis=1, keepdims=True)

    def packed(columns):
        tile = jnp.zeros((act, LANES), jnp.float32)
        for c, column in enumerate(columns):
            tile = jnp.where(lane == c, column, tile)
        return tile

    def spread_columns(mask, columns):
        return [jnp.sum(jnp.where(mask, column, 0.0), axis=0, keepdims=True) for column in columns]

    def spread(mask, tile):
        return spread_columns(mask, [tile[:, c : c + 1] for c in range(6)])

    def targets_of(tile):
        return [jnp.broadcast_to(tile[:, c : c + 1], (act, LANES)) for c in range(6)]

    def zeros():
        return tuple(jnp.zeros((act, LANES), jnp.float32) for _ in range(6))

    def over_bulk(targets, buffer, total, which=None):
        def some(g, total):
            if which is not None:
                await_group(buffer, which, g)
            for i in range(group):
                for start in range(0, part_dev, LANES):
                    k = g * group + i
                    rows = [buffer[k, c : c + 1, start : start + LANES] for c in range(6)]
                    signed = src1[k, 6:7, start : start + LANES]
                    rows.append(jnp.abs(signed) if buffer is src1 else jnp.maximum(signed, 0.0))
                    total = add_pairs(targets, rows, total)
            return total

        return lax.fori_loop(1, chips // group, some, some(0, total))

    blocks = LANES // width
    block = lax.broadcasted_iota(jnp.int32, (2, LANES), 1) // width
    first_block = [lax.rem(chip - i + 4 * chips, group) for i in range(group)]
    masks = [[block == lax.rem(q + first_block[i], blocks) for i in range(group)] for q in range(4)]

    def extra_arrival(first, count, half, g):
        others = extra.at[pl.ds(first, count)]
        return pltpu.make_async_remote_copy(
            src_ref=others, dst_ref=others,
            send_sem=bulk_send.at[2], recv_sem=bulk_recv.at[2 + half, g],
            device_id=partner, device_id_type=MESH,
        )

    def over_extra(targets, total):
        groups = chips // group

        def some(g, total):
            if isinstance(g, int):
                if group > 1:
                    extra_arrival(1, group - 1, 0, g).wait_recv()
            else:
                extra_arrival(g * group, group, 0, g).wait_recv()
            extra_arrival(chips + g * group, group, 1, g).wait_recv()
            slots = [extra[g * group + i] + extra[chips + g * group + i] for i in range(group)]
            rows = [None] * 8
            for q in range(4):
                both = jnp.where(masks[q][0], slots[0], 0.0)
                for i in range(1, group):
                    both = jnp.where(masks[q][i], slots[i], both)
                if q > 0:
                    both = pltpu.roll(both, LANES - q * width, 1)
                rows[q], rows[q + 4] = both[0:1], both[1:2]
            return add_pairs(targets, rows, total)

        return some(0, lax.fori_loop(1, groups, lambda i, t: some(groups - i, t), total))

    def columns_of(total):
        return [jnp.sum(part, axis=1, keepdims=True) for part in total]

    def reduced(total):
        return packed(columns_of(total))

    picker_one = picker_of(place_one, list_one)
    tgt1[0] = packed(
        [picked(picker_one, pred_pos[c : c + 1]) for c in range(3)]
        + [picked(picker_one, pred_vel[c : c + 1]) for c in range(3)]
    )
    pl.semaphore_wait(barrier, 2 * chips - 1)
    to_pair_one = pair_copy(tgt1, 0)
    to_pair_one.start()
    send_bulk(src1, 0)
    to_pair_one.wait_recv()
    late_pos, late_vel = predict(pos, vel, acc, jerk, 2 * STEP_BASE)
    src2[0, 0:3, :] = late_pos
    src2[0, 3:6, :] = late_vel
    picker_two = picker_of(place_two, list_two)
    window = lane == sub_row + lax.rem(chip, group) * width

    def in_slots(column):
        return jnp.sum(jnp.where(window, column, 0.0), axis=0, keepdims=True)

    slot_state = [
        [in_slots(picked(picker_one, rows[c : c + 1])) for c in range(3)]
        for rows in (pos, vel, acc, jerk)
    ]
    slot_mass = in_slots(picked(picker_one, mass))
    send_bulk(src2, 1)
    targets = targets_of(tgt1[0] + tgt1[1])
    partial = columns_of(over_bulk(targets, src1, zeros(), 0))
    part1[0] = packed(partial)
    sums_one = pair_copy(part1, 1)
    sums_one.start()

    rows = spread_columns(window, partial)
    moved = [None] * 8
    for c in range(3):
        state = correct(
            slot_state[0][c], slot_state[1][c], slot_state[2][c], slot_state[3][c],
            rows[c], rows[c + 3], STEP_BASE, True,
        )
        moved[c], moved[c + 3] = predict(*state, STEP_BASE)
    moved[6], moved[7] = slot_mass, jnp.zeros_like(slot_mass)
    for r in range(2):
        line = moved[4 * r]
        for q in range(1, 4):
            line = line + pltpu.roll(jnp.broadcast_to(moved[4 * r + q], (8, LANES)), q * width, 1)[0:1]
        extra[0, r : r + 1, :] = line
    send_extra()

    sums_one.wait_recv()
    force_one = part1[0] + part1[1]
    rows = spread(picker_one, force_one)
    new_acc, new_jerk = jnp.concatenate(rows[0:3], axis=0), jnp.concatenate(rows[3:6], axis=0)
    pos, vel, acc, jerk = correct(pos, vel, acc, jerk, new_acc, new_jerk, stride, hit_one)

    elapsed = jnp.where(hit_one, STEP_BASE, 2 * STEP_BASE)
    pred_pos, pred_vel = predict(pos, vel, acc, jerk, elapsed)
    tgt2[0] = packed(
        [picked(picker_two, pred_pos[c : c + 1]) for c in range(3)]
        + [picked(picker_two, pred_vel[c : c + 1]) for c in range(3)]
    )
    to_pair_two = pair_copy(tgt2, 2)
    to_pair_two.start()
    for c, row in enumerate(spread(place_one, force_one)):
        fresh_o[c, 0:1, :] = row[:, 0:act]
    own_targets = targets_of(tgt2[0])
    own_total = over_bulk(own_targets, src2, zeros(), 1)
    to_pair_two.wait_recv()
    part2[0] = reduced(over_bulk(targets_of(tgt2[1]), src2, zeros()))
    sums_two = pair_copy(part2, 3)
    sums_two.start()
    own = reduced(over_extra(own_targets, own_total))
    sums_two.wait_recv()
    force_two = own + part2[1]
    rows = spread(picker_two, force_two)
    new_acc, new_jerk = jnp.concatenate(rows[0:3], axis=0), jnp.concatenate(rows[3:6], axis=0)
    pos, vel, acc, jerk = correct(pos, vel, acc, jerk, new_acc, new_jerk, stride, hit_two)
    pos_o[...] = pos
    vel_o[...] = vel
    acc_o[...] = acc
    jerk_o[...] = jerk
    for c, row in enumerate(spread(place_two, force_two)):
        fresh_o[c, 1:2, :] = row[:, 0:act]

    extra_arrival(1, 2 * chips - 1, 0, 0).wait_send()
    for which, buffer in enumerate((src1, src2)):
        arrival(buffer, which, 1, chips - 1, 0).wait_send()
    for copy in (to_pair_one, sums_one, to_pair_two, sums_two):
        copy.wait_send()


def write_out(*refs):
    sems = refs[10]
    copies = [pltpu.make_async_copy(refs[i], refs[5 + i], sems.at[i]) for i in range(5)]
    for copy in copies:
        copy.start()
    for copy in copies:
        copy.wait()


def body(n_blk, n_grp, positions, velocities, accelerations, jerks, mass_weight, levels, active, counts):
    part_dev, act = positions.shape[1], active.shape[1]
    chips = n_blk * n_grp // 2
    state = pltpu.VMEM((3, part_dev), jnp.float32)
    vmem = pltpu.VMEM
    results = pl.pallas_call(
        functools.partial(kernel, n_blk, n_grp, act),
        out_shape=(state, state, state, state, pltpu.VMEM((6, 2, act), jnp.float32)),
        in_specs=[pl.BlockSpec(memory_space=pltpu.HBM)] * 8,
        out_specs=[pl.BlockSpec(memory_space=vmem)] * 5,
        scratch_shapes=[
            vmem((3, part_dev), jnp.float32),
            vmem((3, part_dev), jnp.float32),
            vmem((3, part_dev), jnp.float32),
            vmem((3, part_dev), jnp.float32),
            vmem((1, part_dev), jnp.float32),
            vmem((1, part_dev), jnp.int32),
            vmem((2, act), jnp.int32),
            vmem((1, 2), jnp.int32),
            vmem((chips, 7, part_dev), jnp.float32),
            vmem((chips, 6, part_dev), jnp.float32),
            vmem((2 * chips, 2, LANES), jnp.float32),
            vmem((2, act, LANES), jnp.float32),
            vmem((2, act, LANES), jnp.float32),
            vmem((2, act, LANES), jnp.float32),
            vmem((2, act, LANES), jnp.float32),
            pltpu.SemaphoreType.DMA((8,)),
            pltpu.SemaphoreType.DMA((3,)),
            pltpu.SemaphoreType.DMA((4, chips)),
            pltpu.SemaphoreType.DMA((4,)),
            pltpu.SemaphoreType.DMA((4,)),
        ],
        compiler_params=pltpu.CompilerParams(
            collective_id=0, has_side_effects=True, vmem_limit_bytes=32 * 1024 * 1024
        ),
    )(*[pltpu.with_memory_space_constraint(value, pltpu.HBM) for value in (
        positions, velocities, accelerations, jerks,
        mass_weight.reshape(1, part_dev), levels.reshape(1, part_dev), active, counts.reshape(1, 2),
    )])
    written = pl.pallas_call(
        write_out,
        out_shape=[jax.ShapeDtypeStruct(r.shape, r.dtype) for r in results],
        in_specs=[pl.BlockSpec(memory_space=vmem)] * 5,
        out_specs=[pl.BlockSpec(memory_space=pltpu.HBM)] * 5,
        scratch_shapes=[pltpu.SemaphoreType.DMA((5,))],
        compiler_params=pltpu.CompilerParams(vmem_limit_bytes=1024 * 1024),
    )(*[pltpu.with_memory_space_constraint(value, vmem) for value in results])
    return (*written[0:4], written[4].transpose(1, 0, 2))


def solution(mesh):
    spread_over = ("blk", "grp")
    in_specs = (
        P(None, spread_over),
        P(None, spread_over),
        P(None, spread_over),
        P(None, spread_over),
        P(spread_over),
        P(spread_over),
        P(None, spread_over),
        P(None, spread_over),
    )
    out_specs = (
        P(None, spread_over),
        P(None, spread_over),
        P(None, spread_over),
        P(None, spread_over),
        P(None, None, spread_over),
    )
    inner = functools.partial(body, mesh.shape["blk"], mesh.shape["grp"])
    return jax.shard_map(inner, mesh=mesh, in_specs=in_specs, out_specs=out_specs, check_vma=False)
```

```python
import functools
import math

import jax
import jax.numpy as jnp
from jax import lax
from jax.experimental import pallas as pl
from jax.experimental.pallas import tpu as pltpu
from jax.sharding import PartitionSpec as P

STEP_BASE = 0.125
SOFTEN = 0.01
LANES = 128
MESH = pl.DeviceIdType.MESH


def predict(pos, vel, acc, jerk, elapsed):
    pred_pos = pos + elapsed * (vel + elapsed * (acc * 0.5 + elapsed * jerk / 6.0))
    pred_vel = vel + elapsed * (acc + elapsed * jerk * 0.5)
    return (pred_pos, pred_vel)


def correct(pos, vel, acc, jerk, new_acc, new_jerk, stride, hit):
    half = 0.5 * stride
    square = stride * stride / 12.0
    vel_new = vel + half * (acc + new_acc) + square * (jerk - new_jerk)
    pos_new = pos + half * (vel + vel_new) + square * (acc - new_acc)
    return (
        jnp.where(hit, pos_new, pos),
        jnp.where(hit, vel_new, vel),
        jnp.where(hit, new_acc, acc),
        jnp.where(hit, new_jerk, jerk),
    )


def add_pairs(target, source, total):
    dpos = [source[c] - target[c] for c in range(3)]
    dvel = [source[c + 3] - target[c + 3] for c in range(3)]
    dist = dpos[0] * dpos[0] + dpos[1] * dpos[1] + dpos[2] * dpos[2] + SOFTEN
    inverse = lax.rsqrt(dist)
    square = inverse * inverse
    weight = source[6] * (inverse * square)
    radial = (3.0 * square) * (dpos[0] * dvel[0] + dpos[1] * dvel[1] + dpos[2] * dvel[2])
    accel = [total[c] + weight * dpos[c] for c in range(3)]
    jerk = [total[c + 3] + weight * (dvel[c] - radial * dpos[c]) for c in range(3)]
    return tuple(accel + jerk)


def kernel(
    n_blk, n_grp, act,
    pos_h, vel_h, acc_h, jerk_h, mass_h, lev_h, lists_h, counts_h,
    pos_o, vel_o, acc_o, jerk_o, fresh_o,
    pos_v, vel_v, acc_v, jerk_v, mass_v, lev_v, lists_v, counts_v,
    src1, src2, extra, tgt1, tgt2, part1, part2,
    load_sem, bulk_send, bulk_recv, pair_send, pair_recv,
):
    blk, grp = lax.axis_index("blk"), lax.axis_index("grp")
    per_blk = n_grp // 2
    chips = n_blk * per_blk
    core = lax.rem(grp, 2)
    chip = blk * per_blk + grp // 2
    partner = (blk, grp + 1 - 2 * core)
    part_dev = pos_h.shape[1]
    total_part = part_dev * n_blk * n_grp
    width = 1 << (act - 1).bit_length()
    group = math.gcd(LANES // width, chips)

    def device_at(there, which_core):
        return (there // per_blk, 2 * lax.rem(there, per_blk) + which_core)

    def far_first(visit):
        def turn(j, carry):
            step = ((j + 1) // 2) * (1 - 2 * lax.rem(j, 2))
            there = lax.rem(3 * chips - 1 + step - chip, chips)
            visit(there, lax.rem(there - chip + chips, chips))
            return carry

        lax.fori_loop(0, chips, turn, 0)

    loads = [
        pltpu.make_async_copy(h, v, load_sem.at[i])
        for i, (h, v) in enumerate(
            [(pos_h, pos_v), (vel_h, vel_v), (acc_h, acc_v), (jerk_h, jerk_v),
             (mass_h, mass_v), (lev_h, lev_v), (lists_h, lists_v), (counts_h, counts_v)]
        )
    ]

    barrier = pltpu.get_barrier_semaphore()

    def greet(there, k):
        def signal(which_core):
            pl.semaphore_signal(barrier, inc=1, device_id=device_at(there, which_core), device_id_type=MESH)

        pl.when(k != 0)(lambda: signal(core))
        signal(1 - core)

    far_first(greet)
    for load in loads:
        load.start()

    def send_bulk(buffer, which):
        def send(there, k):
            @pl.when(k != 0)
            def _():
                pltpu.make_async_remote_copy(
                    src_ref=buffer.at[0], dst_ref=buffer.at[k],
                    send_sem=bulk_send.at[which], recv_sem=bulk_recv.at[which, k // group],
                    device_id=device_at(there, core), device_id_type=MESH,
                ).start()

        far_first(send)

    def send_extra():
        def send(there, k):
            def copy(half, which_core):
                pltpu.make_async_remote_copy(
                    src_ref=extra.at[0], dst_ref=extra.at[half * chips + k],
                    send_sem=bulk_send.at[2], recv_sem=bulk_recv.at[2 + half, k // group],
                    device_id=device_at(there, which_core), device_id_type=MESH,
                ).start()

            pl.when(k != 0)(lambda: copy(0, core))
            copy(1, 1 - core)

        far_first(send)

    def arrival(buffer, which, first, count, sems):
        others = buffer.at[pl.ds(first, count)]
        return pltpu.make_async_remote_copy(
            src_ref=others, dst_ref=others,
            send_sem=bulk_send.at[which], recv_sem=bulk_recv.at[which, sems],
            device_id=partner, device_id_type=MESH,
        )

    def await_group(buffer, which, g):
        if isinstance(g, int) and g == 0:
            if group > 1:
                arrival(buffer, which, 1, group - 1, 0).wait_recv()
        else:
            arrival(buffer, which, g * group, group, g).wait_recv()

    def pair_copy(buffer, which):
        return pltpu.make_async_remote_copy(
            src_ref=buffer.at[0], dst_ref=buffer.at[1],
            send_sem=pair_send.at[which], recv_sem=pair_recv.at[which],
            device_id=partner, device_id_type=MESH,
        )

    for load in loads:
        load.wait()
    pos, vel, acc, jerk = pos_v[...], vel_v[...], acc_v[...], jerk_v[...]
    mass = mass_v[...] / total_part
    levels = lev_v[...]
    stride = STEP_BASE * jnp.left_shift(jnp.ones_like(levels), levels).astype(jnp.float32)
    hit_one, hit_two = levels == 0, levels <= 1
    pred_pos, pred_vel = predict(pos, vel, acc, jerk, STEP_BASE)
    src1[0, 0:3, :] = pred_pos
    src1[0, 3:6, :] = pred_vel
    src1[0, 6:7, :] = jnp.where(hit_one, -mass, mass)

    sub_row = lax.broadcasted_iota(jnp.int32, (act, LANES), 0)
    lane = lax.broadcasted_iota(jnp.int32, (act, LANES), 1)
    particle = lax.broadcasted_iota(jnp.int32, (act, part_dev), 1)
    count_one = jnp.broadcast_to(counts_v[0:1, 0:1], (act, LANES))
    count_two = jnp.broadcast_to(counts_v[0:1, 1:2], (act, LANES))
    list_one = jnp.concatenate([lists_v[0:1, :], jnp.zeros((1, LANES - act), jnp.int32)], axis=1)
    list_two = jnp.concatenate([lists_v[1:2, :], jnp.zeros((1, LANES - act), jnp.int32)], axis=1)
    shift = core * (act - count_one)
    place_one = (lane == sub_row - shift) & (lane < count_one)
    place_two = (lane == sub_row) & (lane < count_two)

    def picker_of(place, row):
        value = jnp.where(place, (row + 1).astype(jnp.float32), 0.0)
        column = jnp.sum(value, axis=1, keepdims=True) - 1.0
        return particle.astype(jnp.float32) == column

    def picked(picker, rows):
        return jnp.sum(jnp.where(picker, rows, 0.0), axis=1, keepdims=True)

    def packed(columns):
        tile = jnp.zeros((act, LANES), jnp.float32)
        for c, column in enumerate(columns):
            tile = jnp.where(lane == c, column, tile)
        return tile

    def spread_columns(mask, columns):
        return [jnp.sum(jnp.where(mask, column, 0.0), axis=0, keepdims=True) for column in columns]

    def spread(mask, tile):
        return spread_columns(mask, [tile[:, c : c + 1] for c in range(6)])

    def targets_of(tile):
        return [jnp.broadcast_to(tile[:, c : c + 1], (act, LANES)) for c in range(6)]

    def zeros():
        return tuple(jnp.zeros((act, LANES), jnp.float32) for _ in range(6))

    def over_bulk(targets, buffer, total, which=None, awaited=0):
        def some(g, total):
            if which is not None and not (isinstance(g, int) and g < awaited):
                await_group(buffer, which, g)
            for i in range(group):
                for start in range(0, part_dev, LANES):
                    k = g * group + i
                    rows = [buffer[k, c : c + 1, start : start + LANES] for c in range(6)]
                    signed = src1[k, 6:7, start : start + LANES]
                    rows.append(jnp.abs(signed) if buffer is src1 else jnp.maximum(signed, 0.0))
                    total = add_pairs(targets, rows, total)
            return total

        return lax.fori_loop(1, chips // group, some, some(0, total))

    blocks = LANES // width
    block = lax.broadcasted_iota(jnp.int32, (2, LANES), 1) // width
    first_block = [lax.rem(chip - i + 4 * chips, group) for i in range(group)]
    masks = [[block == lax.rem(q + first_block[i], blocks) for i in range(group)] for q in range(4)]

    def extra_arrival(first, count, half, g):
        others = extra.at[pl.ds(first, count)]
        return pltpu.make_async_remote_copy(
            src_ref=others, dst_ref=others,
            send_sem=bulk_send.at[2], recv_sem=bulk_recv.at[2 + half, g],
            device_id=partner, device_id_type=MESH,
        )

    def over_extra(targets, total):
        groups = chips // group

        def some(g, total):
            if isinstance(g, int):
                if group > 1:
                    extra_arrival(1, group - 1, 0, g).wait_recv()
            else:
                extra_arrival(g * group, group, 0, g).wait_recv()
            extra_arrival(chips + g * group, group, 1, g).wait_recv()
            slots = [extra[g * group + i] + extra[chips + g * group + i] for i in range(group)]
            rows = [None] * 8
            for q in range(4):
                both = jnp.where(masks[q][0], slots[0], 0.0)
                for i in range(1, group):
                    both = jnp.where(masks[q][i], slots[i], both)
                if q > 0:
                    both = pltpu.roll(both, LANES - q * width, 1)
                rows[q], rows[q + 4] = both[0:1], both[1:2]
            return add_pairs(targets, rows, total)

        return some(0, lax.fori_loop(1, groups, lambda i, t: some(groups - i, t), total))

    def columns_of(total):
        return [jnp.sum(part, axis=1, keepdims=True) for part in total]

    def reduced(total):
        return packed(columns_of(total))

    picker_one = picker_of(place_one, list_one)
    tgt1[0] = packed(
        [picked(picker_one, pred_pos[c : c + 1]) for c in range(3)]
        + [picked(picker_one, pred_vel[c : c + 1]) for c in range(3)]
    )
    pl.semaphore_wait(barrier, 2 * chips - 1)
    to_pair_one = pair_copy(tgt1, 0)
    to_pair_one.start()
    send_bulk(src1, 0)
    to_pair_one.wait_recv()
    late_pos, late_vel = predict(pos, vel, acc, jerk, 2 * STEP_BASE)
    src2[0, 0:3, :] = late_pos
    src2[0, 3:6, :] = late_vel
    picker_two = picker_of(place_two, list_two)
    window = lane == sub_row + lax.rem(chip, group) * width

    def in_slots(column):
        return jnp.sum(jnp.where(window, column, 0.0), axis=0, keepdims=True)

    slot_state = [
        [in_slots(picked(picker_one, rows[c : c + 1])) for c in range(3)]
        for rows in (pos, vel, acc, jerk)
    ]
    slot_mass = in_slots(picked(picker_one, mass))
    await_group(src1, 0, 0)
    send_bulk(src2, 1)
    targets = targets_of(tgt1[0] + tgt1[1])
    partial = columns_of(over_bulk(targets, src1, zeros(), 0, 1))
    part1[0] = packed(partial)
    sums_one = pair_copy(part1, 1)
    sums_one.start()

    rows = spread_columns(window, partial)
    moved = [None] * 8
    for c in range(3):
        state = correct(
            slot_state[0][c], slot_state[1][c], slot_state[2][c], slot_state[3][c],
            rows[c], rows[c + 3], STEP_BASE, True,
        )
        moved[c], moved[c + 3] = predict(*state, STEP_BASE)
    moved[6], moved[7] = slot_mass, jnp.zeros_like(slot_mass)
    for r in range(2):
        line = moved[4 * r]
        for q in range(1, 4):
            line = line + pltpu.roll(jnp.broadcast_to(moved[4 * r + q], (8, LANES)), q * width, 1)[0:1]
        extra[0, r : r + 1, :] = line
    send_extra()

    sums_one.wait_recv()
    force_one = part1[0] + part1[1]
    rows = spread(picker_one, force_one)
    new_acc, new_jerk = jnp.concatenate(rows[0:3], axis=0), jnp.concatenate(rows[3:6], axis=0)
    pos, vel, acc, jerk = correct(pos, vel, acc, jerk, new_acc, new_jerk, stride, hit_one)

    elapsed = jnp.where(hit_one, STEP_BASE, 2 * STEP_BASE)
    pred_pos, pred_vel = predict(pos, vel, acc, jerk, elapsed)
    tgt2[0] = packed(
        [picked(picker_two, pred_pos[c : c + 1]) for c in range(3)]
        + [picked(picker_two, pred_vel[c : c + 1]) for c in range(3)]
    )
    to_pair_two = pair_copy(tgt2, 2)
    to_pair_two.start()
    for c, row in enumerate(spread(place_one, force_one)):
        fresh_o[c, 0:1, :] = row[:, 0:act]
    own_targets = targets_of(tgt2[0])
    own_total = over_bulk(own_targets, src2, zeros(), 1)
    to_pair_two.wait_recv()
    part2[0] = reduced(over_bulk(targets_of(tgt2[1]), src2, zeros()))
    sums_two = pair_copy(part2, 3)
    sums_two.start()
    own = reduced(over_extra(own_targets, own_total))
    sums_two.wait_recv()
    force_two = own + part2[1]
    rows = spread(picker_two, force_two)
    new_acc, new_jerk = jnp.concatenate(rows[0:3], axis=0), jnp.concatenate(rows[3:6], axis=0)
    pos, vel, acc, jerk = correct(pos, vel, acc, jerk, new_acc, new_jerk, stride, hit_two)
    pos_o[...] = pos
    vel_o[...] = vel
    acc_o[...] = acc
    jerk_o[...] = jerk
    for c, row in enumerate(spread(place_two, force_two)):
        fresh_o[c, 1:2, :] = row[:, 0:act]

    extra_arrival(1, 2 * chips - 1, 0, 0).wait_send()
    for which, buffer in enumerate((src1, src2)):
        arrival(buffer, which, 1, chips - 1, 0).wait_send()
    for copy in (to_pair_one, sums_one, to_pair_two, sums_two):
        copy.wait_send()


def write_out(*refs):
    sems = refs[10]
    copies = [pltpu.make_async_copy(refs[i], refs[5 + i], sems.at[i]) for i in range(5)]
    for copy in copies:
        copy.start()
    for copy in copies:
        copy.wait()


def body(n_blk, n_grp, positions, velocities, accelerations, jerks, mass_weight, levels, active, counts):
    part_dev, act = positions.shape[1], active.shape[1]
    chips = n_blk * n_grp // 2
    state = pltpu.VMEM((3, part_dev), jnp.float32)
    vmem = pltpu.VMEM
    results = pl.pallas_call(
        functools.partial(kernel, n_blk, n_grp, act),
        out_shape=(state, state, state, state, pltpu.VMEM((6, 2, act), jnp.float32)),
        in_specs=[pl.BlockSpec(memory_space=pltpu.HBM)] * 8,
        out_specs=[pl.BlockSpec(memory_space=vmem)] * 5,
        scratch_shapes=[
            vmem((3, part_dev), jnp.float32),
            vmem((3, part_dev), jnp.float32),
            vmem((3, part_dev), jnp.float32),
            vmem((3, part_dev), jnp.float32),
            vmem((1, part_dev), jnp.float32),
            vmem((1, part_dev), jnp.int32),
            vmem((2, act), jnp.int32),
            vmem((1, 2), jnp.int32),
            vmem((chips, 7, part_dev), jnp.float32),
            vmem((chips, 6, part_dev), jnp.float32),
            vmem((2 * chips, 2, LANES), jnp.float32),
            vmem((2, act, LANES), jnp.float32),
            vmem((2, act, LANES), jnp.float32),
            vmem((2, act, LANES), jnp.float32),
            vmem((2, act, LANES), jnp.float32),
            pltpu.SemaphoreType.DMA((8,)),
            pltpu.SemaphoreType.DMA((3,)),
            pltpu.SemaphoreType.DMA((4, chips)),
            pltpu.SemaphoreType.DMA((4,)),
            pltpu.SemaphoreType.DMA((4,)),
        ],
        compiler_params=pltpu.CompilerParams(
            collective_id=0, has_side_effects=True, vmem_limit_bytes=32 * 1024 * 1024
        ),
    )(*[pltpu.with_memory_space_constraint(value, pltpu.HBM) for value in (
        positions, velocities, accelerations, jerks,
        mass_weight.reshape(1, part_dev), levels.reshape(1, part_dev), active, counts.reshape(1, 2),
    )])
    written = pl.pallas_call(
        write_out,
        out_shape=[jax.ShapeDtypeStruct(r.shape, r.dtype) for r in results],
        in_specs=[pl.BlockSpec(memory_space=vmem)] * 5,
        out_specs=[pl.BlockSpec(memory_space=pltpu.HBM)] * 5,
        scratch_shapes=[pltpu.SemaphoreType.DMA((5,))],
        compiler_params=pltpu.CompilerParams(vmem_limit_bytes=1024 * 1024),
    )(*[pltpu.with_memory_space_constraint(value, vmem) for value in results])
    return (*written[0:4], written[4].transpose(1, 0, 2))


def solution(mesh):
    spread_over = ("blk", "grp")
    in_specs = (
        P(None, spread_over),
        P(None, spread_over),
        P(None, spread_over),
        P(None, spread_over),
        P(spread_over),
        P(spread_over),
        P(None, spread_over),
        P(None, spread_over),
    )
    out_specs = (
        P(None, spread_over),
        P(None, spread_over),
        P(None, spread_over),
        P(None, spread_over),
        P(None, None, spread_over),
    )
    inner = functools.partial(body, mesh.shape["blk"], mesh.shape["grp"])
    return jax.shard_map(inner, mesh=mesh, in_specs=in_specs, out_specs=out_specs, check_vma=False)
```

```python
import functools
import math

import jax
import jax.numpy as jnp
from jax import lax
from jax.experimental import pallas as pl
from jax.experimental.pallas import tpu as pltpu
from jax.sharding import PartitionSpec as P

STEP_BASE = 0.125
SOFTEN = 0.01
LANES = 128
MESH = pl.DeviceIdType.MESH


def predict(pos, vel, acc, jerk, elapsed):
    pred_pos = pos + elapsed * (vel + elapsed * (acc * 0.5 + elapsed * jerk / 6.0))
    pred_vel = vel + elapsed * (acc + elapsed * jerk * 0.5)
    return (pred_pos, pred_vel)


def correct(pos, vel, acc, jerk, new_acc, new_jerk, stride, hit):
    half = 0.5 * stride
    square = stride * stride / 12.0
    vel_new = vel + half * (acc + new_acc) + square * (jerk - new_jerk)
    pos_new = pos + half * (vel + vel_new) + square * (acc - new_acc)
    return (
        jnp.where(hit, pos_new, pos),
        jnp.where(hit, vel_new, vel),
        jnp.where(hit, new_acc, acc),
        jnp.where(hit, new_jerk, jerk),
    )


def add_pairs(target, source, total):
    dpos = [source[c] - target[c] for c in range(3)]
    dvel = [source[c + 3] - target[c + 3] for c in range(3)]
    dist = dpos[0] * dpos[0] + dpos[1] * dpos[1] + dpos[2] * dpos[2] + SOFTEN
    inverse = lax.rsqrt(dist)
    square = inverse * inverse
    weight = source[6] * (inverse * square)
    radial = (3.0 * square) * (dpos[0] * dvel[0] + dpos[1] * dvel[1] + dpos[2] * dvel[2])
    accel = [total[c] + weight * dpos[c] for c in range(3)]
    jerk = [total[c + 3] + weight * (dvel[c] - radial * dpos[c]) for c in range(3)]
    return tuple(accel + jerk)


def kernel(
    n_blk, n_grp, act,
    pos_h, vel_h, acc_h, jerk_h, mass_h, lev_h, lists_h, counts_h,
    pos_o, vel_o, acc_o, jerk_o, fresh_o,
    pos_v, vel_v, acc_v, jerk_v, mass_v, lev_v, lists_v, counts_v,
    src1, src2, extra, tgt1, tgt2, part1, part2,
    load_sem, bulk_send, bulk_recv, pair_send, pair_recv,
):
    blk, grp = lax.axis_index("blk"), lax.axis_index("grp")
    per_blk = n_grp // 2
    chips = n_blk * per_blk
    core = lax.rem(grp, 2)
    chip = blk * per_blk + grp // 2
    partner = (blk, grp + 1 - 2 * core)
    part_dev = pos_h.shape[1]
    total_part = part_dev * n_blk * n_grp
    width = 1 << (act - 1).bit_length()
    group = math.gcd(LANES // width, chips)

    def device_at(there, which_core):
        return (there // per_blk, 2 * lax.rem(there, per_blk) + which_core)

    def far_first(visit):
        def turn(j, carry):
            step = ((j + 1) // 2) * (1 - 2 * lax.rem(j, 2))
            there = lax.rem(3 * chips - 1 + step - chip, chips)
            visit(there, lax.rem(there - chip + chips, chips))
            return carry

        lax.fori_loop(0, chips, turn, 0)

    loads = [
        pltpu.make_async_copy(h, v, load_sem.at[i])
        for i, (h, v) in enumerate(
            [(pos_h, pos_v), (vel_h, vel_v), (acc_h, acc_v), (jerk_h, jerk_v),
             (mass_h, mass_v), (lev_h, lev_v), (lists_h, lists_v), (counts_h, counts_v)]
        )
    ]

    barrier = pltpu.get_barrier_semaphore()

    def greet(there, k):
        def signal(which_core):
            pl.semaphore_signal(barrier, inc=1, device_id=device_at(there, which_core), device_id_type=MESH)

        pl.when(k != 0)(lambda: signal(core))
        signal(1 - core)

    far_first(greet)
    for load in loads:
        load.start()

    def send_bulk(buffer, which):
        def send(there, k):
            @pl.when(k != 0)
            def _():
                pltpu.make_async_remote_copy(
                    src_ref=buffer.at[0], dst_ref=buffer.at[k],
                    send_sem=bulk_send.at[which], recv_sem=bulk_recv.at[which, k // group],
                    device_id=device_at(there, core), device_id_type=MESH,
                ).start()

        far_first(send)

    def send_extra():
        def send(there, k):
            def copy(half, which_core):
                pltpu.make_async_remote_copy(
                    src_ref=extra.at[0], dst_ref=extra.at[half * chips + k],
                    send_sem=bulk_send.at[2], recv_sem=bulk_recv.at[2 + half, k // group],
                    device_id=device_at(there, which_core), device_id_type=MESH,
                ).start()

            pl.when(k != 0)(lambda: copy(0, core))
            copy(1, 1 - core)

        far_first(send)

    def arrival(buffer, which, first, count, sems):
        others = buffer.at[pl.ds(first, count)]
        return pltpu.make_async_remote_copy(
            src_ref=others, dst_ref=others,
            send_sem=bulk_send.at[which], recv_sem=bulk_recv.at[which, sems],
            device_id=partner, device_id_type=MESH,
        )

    def await_group(buffer, which, g):
        if isinstance(g, int) and g == 0:
            if group > 1:
                arrival(buffer, which, 1, group - 1, 0).wait_recv()
        else:
            arrival(buffer, which, g * group, group, g).wait_recv()

    def pair_copy(buffer, which):
        return pltpu.make_async_remote_copy(
            src_ref=buffer.at[0], dst_ref=buffer.at[1],
            send_sem=pair_send.at[which], recv_sem=pair_recv.at[which],
            device_id=partner, device_id_type=MESH,
        )

    for load in loads:
        load.wait()
    pos, vel, acc, jerk = pos_v[...], vel_v[...], acc_v[...], jerk_v[...]
    mass = mass_v[...] / total_part
    levels = lev_v[...]
    stride = STEP_BASE * jnp.left_shift(jnp.ones_like(levels), levels).astype(jnp.float32)
    hit_one, hit_two = levels == 0, levels <= 1
    pred_pos, pred_vel = predict(pos, vel, acc, jerk, STEP_BASE)
    src1[0, 0:3, :] = pred_pos
    src1[0, 3:6, :] = pred_vel
    src1[0, 6:7, :] = jnp.where(hit_one, -mass, mass)

    sub_row = lax.broadcasted_iota(jnp.int32, (act, LANES), 0)
    lane = lax.broadcasted_iota(jnp.int32, (act, LANES), 1)
    particle = lax.broadcasted_iota(jnp.int32, (act, part_dev), 1)
    count_one = jnp.broadcast_to(counts_v[0:1, 0:1], (act, LANES))
    count_two = jnp.broadcast_to(counts_v[0:1, 1:2], (act, LANES))
    list_one = jnp.concatenate([lists_v[0:1, :], jnp.zeros((1, LANES - act), jnp.int32)], axis=1)
    list_two = jnp.concatenate([lists_v[1:2, :], jnp.zeros((1, LANES - act), jnp.int32)], axis=1)
    shift = core * (act - count_one)
    place_one = (lane == sub_row - shift) & (lane < count_one)
    place_two = (lane == sub_row) & (lane < count_two)

    def picker_of(place, row):
        value = jnp.where(place, (row + 1).astype(jnp.float32), 0.0)
        column = jnp.sum(value, axis=1, keepdims=True) - 1.0
        return particle.astype(jnp.float32) == column

    def picked(picker, rows):
        return jnp.sum(jnp.where(picker, rows, 0.0), axis=1, keepdims=True)

    def packed(columns):
        tile = jnp.zeros((act, LANES), jnp.float32)
        for c, column in enumerate(columns):
            tile = jnp.where(lane == c, column, tile)
        return tile

    def spread_columns(mask, columns):
        return [jnp.sum(jnp.where(mask, column, 0.0), axis=0, keepdims=True) for column in columns]

    def spread(mask, tile):
        return spread_columns(mask, [tile[:, c : c + 1] for c in range(6)])

    def targets_of(tile):
        return [jnp.broadcast_to(tile[:, c : c + 1], (act, LANES)) for c in range(6)]

    def zeros():
        return tuple(jnp.zeros((act, LANES), jnp.float32) for _ in range(6))

    def over_bulk(targets, buffer, total, which=None, awaited=0):
        def some(g, total):
            if which is not None and not (isinstance(g, int) and g < awaited):
                await_group(buffer, which, g)
            for i in range(group):
                for start in range(0, part_dev, LANES):
                    k = g * group + i
                    rows = [buffer[k, c : c + 1, start : start + LANES] for c in range(6)]
                    signed = src1[k, 6:7, start : start + LANES]
                    rows.append(jnp.abs(signed) if buffer is src1 else jnp.maximum(signed, 0.0))
                    total = add_pairs(targets, rows, total)
            return total

        return lax.fori_loop(1, chips // group, some, some(0, total))

    blocks = LANES // width
    block = lax.broadcasted_iota(jnp.int32, (2, LANES), 1) // width
    first_block = [lax.rem(chip - i + 4 * chips, group) for i in range(group)]
    masks = [[block == lax.rem(q + first_block[i], blocks) for i in range(group)] for q in range(4)]

    def extra_arrival(first, count, half, g):
        others = extra.at[pl.ds(first, count)]
        return pltpu.make_async_remote_copy(
            src_ref=others, dst_ref=others,
            send_sem=bulk_send.at[2], recv_sem=bulk_recv.at[2 + half, g],
            device_id=partner, device_id_type=MESH,
        )

    def over_extra(targets, total):
        groups = chips // group

        def some(g, total):
            if isinstance(g, int):
                if group > 1:
                    extra_arrival(1, group - 1, 0, g).wait_recv()
            else:
                extra_arrival(g * group, group, 0, g).wait_recv()
            extra_arrival(chips + g * group, group, 1, g).wait_recv()
            slots = [extra[g * group + i] + extra[chips + g * group + i] for i in range(group)]
            rows = [None] * 8
            for q in range(4):
                both = jnp.where(masks[q][0], slots[0], 0.0)
                for i in range(1, group):
                    both = jnp.where(masks[q][i], slots[i], both)
                if q > 0:
                    both = pltpu.roll(both, LANES - q * width, 1)
                rows[q], rows[q + 4] = both[0:1], both[1:2]
            return add_pairs(targets, rows, total)

        return some(0, lax.fori_loop(1, groups, lambda i, t: some(groups - i, t), total))

    def columns_of(total):
        return [jnp.sum(part, axis=1, keepdims=True) for part in total]

    def reduced(total):
        return packed(columns_of(total))

    picker_one = picker_of(place_one, list_one)
    tgt1[0] = packed(
        [picked(picker_one, pred_pos[c : c + 1]) for c in range(3)]
        + [picked(picker_one, pred_vel[c : c + 1]) for c in range(3)]
    )
    pl.semaphore_wait(barrier, 2 * chips - 1)
    to_pair_one = pair_copy(tgt1, 0)
    to_pair_one.start()
    send_bulk(src1, 0)
    to_pair_one.wait_recv()
    late_pos, late_vel = predict(pos, vel, acc, jerk, 2 * STEP_BASE)
    src2[0, 0:3, :] = late_pos
    src2[0, 3:6, :] = late_vel
    picker_two = picker_of(place_two, list_two)
    window = lane == sub_row + lax.rem(chip, group) * width

    def in_slots(column):
        return jnp.sum(jnp.where(window, column, 0.0), axis=0, keepdims=True)

    slot_state = [
        [in_slots(picked(picker_one, rows[c : c + 1])) for c in range(3)]
        for rows in (pos, vel, acc, jerk)
    ]
    slot_mass = in_slots(picked(picker_one, mass))
    early = lax.rem(chip, per_blk) < per_blk // 4
    pl.when(early)(lambda: send_bulk(src2, 1))
    await_group(src1, 0, 0)
    pl.when(jnp.logical_not(early))(lambda: send_bulk(src2, 1))
    targets = targets_of(tgt1[0] + tgt1[1])
    partial = columns_of(over_bulk(targets, src1, zeros(), 0, 1))
    part1[0] = packed(partial)
    sums_one = pair_copy(part1, 1)
    sums_one.start()

    rows = spread_columns(window, partial)
    moved = [None] * 8
    for c in range(3):
        state = correct(
            slot_state[0][c], slot_state[1][c], slot_state[2][c], slot_state[3][c],
            rows[c], rows[c + 3], STEP_BASE, True,
        )
        moved[c], moved[c + 3] = predict(*state, STEP_BASE)
    moved[6], moved[7] = slot_mass, jnp.zeros_like(slot_mass)
    for r in range(2):
        line = moved[4 * r]
        for q in range(1, 4):
            line = line + pltpu.roll(jnp.broadcast_to(moved[4 * r + q], (8, LANES)), q * width, 1)[0:1]
        extra[0, r : r + 1, :] = line
    send_extra()

    sums_one.wait_recv()
    force_one = part1[0] + part1[1]
    rows = spread(picker_one, force_one)
    new_acc, new_jerk = jnp.concatenate(rows[0:3], axis=0), jnp.concatenate(rows[3:6], axis=0)
    pos, vel, acc, jerk = correct(pos, vel, acc, jerk, new_acc, new_jerk, stride, hit_one)

    elapsed = jnp.where(hit_one, STEP_BASE, 2 * STEP_BASE)
    pred_pos, pred_vel = predict(pos, vel, acc, jerk, elapsed)
    tgt2[0] = packed(
        [picked(picker_two, pred_pos[c : c + 1]) for c in range(3)]
        + [picked(picker_two, pred_vel[c : c + 1]) for c in range(3)]
    )
    to_pair_two = pair_copy(tgt2, 2)
    to_pair_two.start()
    for c, row in enumerate(spread(place_one, force_one)):
        fresh_o[c, 0:1, :] = row[:, 0:act]
    own_targets = targets_of(tgt2[0])
    own_total = over_bulk(own_targets, src2, zeros(), 1)
    to_pair_two.wait_recv()
    part2[0] = reduced(over_bulk(targets_of(tgt2[1]), src2, zeros()))
    sums_two = pair_copy(part2, 3)
    sums_two.start()
    own = reduced(over_extra(own_targets, own_total))
    sums_two.wait_recv()
    force_two = own + part2[1]
    rows = spread(picker_two, force_two)
    new_acc, new_jerk = jnp.concatenate(rows[0:3], axis=0), jnp.concatenate(rows[3:6], axis=0)
    pos, vel, acc, jerk = correct(pos, vel, acc, jerk, new_acc, new_jerk, stride, hit_two)
    pos_o[...] = pos
    vel_o[...] = vel
    acc_o[...] = acc
    jerk_o[...] = jerk
    for c, row in enumerate(spread(place_two, force_two)):
        fresh_o[c, 1:2, :] = row[:, 0:act]

    extra_arrival(1, 2 * chips - 1, 0, 0).wait_send()
    for which, buffer in enumerate((src1, src2)):
        arrival(buffer, which, 1, chips - 1, 0).wait_send()
    for copy in (to_pair_one, sums_one, to_pair_two, sums_two):
        copy.wait_send()


def write_out(*refs):
    sems = refs[10]
    copies = [pltpu.make_async_copy(refs[i], refs[5 + i], sems.at[i]) for i in range(5)]
    for copy in copies:
        copy.start()
    for copy in copies:
        copy.wait()


def body(n_blk, n_grp, positions, velocities, accelerations, jerks, mass_weight, levels, active, counts):
    part_dev, act = positions.shape[1], active.shape[1]
    chips = n_blk * n_grp // 2
    state = pltpu.VMEM((3, part_dev), jnp.float32)
    vmem = pltpu.VMEM
    results = pl.pallas_call(
        functools.partial(kernel, n_blk, n_grp, act),
        out_shape=(state, state, state, state, pltpu.VMEM((6, 2, act), jnp.float32)),
        in_specs=[pl.BlockSpec(memory_space=pltpu.HBM)] * 8,
        out_specs=[pl.BlockSpec(memory_space=vmem)] * 5,
        scratch_shapes=[
            vmem((3, part_dev), jnp.float32),
            vmem((3, part_dev), jnp.float32),
            vmem((3, part_dev), jnp.float32),
            vmem((3, part_dev), jnp.float32),
            vmem((1, part_dev), jnp.float32),
            vmem((1, part_dev), jnp.int32),
            vmem((2, act), jnp.int32),
            vmem((1, 2), jnp.int32),
            vmem((chips, 7, part_dev), jnp.float32),
            vmem((chips, 6, part_dev), jnp.float32),
            vmem((2 * chips, 2, LANES), jnp.float32),
            vmem((2, act, LANES), jnp.float32),
            vmem((2, act, LANES), jnp.float32),
            vmem((2, act, LANES), jnp.float32),
            vmem((2, act, LANES), jnp.float32),
            pltpu.SemaphoreType.DMA((8,)),
            pltpu.SemaphoreType.DMA((3,)),
            pltpu.SemaphoreType.DMA((4, chips)),
            pltpu.SemaphoreType.DMA((4,)),
            pltpu.SemaphoreType.DMA((4,)),
        ],
        compiler_params=pltpu.CompilerParams(
            collective_id=0, has_side_effects=True, vmem_limit_bytes=32 * 1024 * 1024
        ),
    )(*[pltpu.with_memory_space_constraint(value, pltpu.HBM) for value in (
        positions, velocities, accelerations, jerks,
        mass_weight.reshape(1, part_dev), levels.reshape(1, part_dev), active, counts.reshape(1, 2),
    )])
    written = pl.pallas_call(
        write_out,
        out_shape=[jax.ShapeDtypeStruct(r.shape, r.dtype) for r in results],
        in_specs=[pl.BlockSpec(memory_space=vmem)] * 5,
        out_specs=[pl.BlockSpec(memory_space=pltpu.HBM)] * 5,
        scratch_shapes=[pltpu.SemaphoreType.DMA((5,))],
        compiler_params=pltpu.CompilerParams(vmem_limit_bytes=1024 * 1024),
    )(*[pltpu.with_memory_space_constraint(value, vmem) for value in results])
    return (*written[0:4], written[4].transpose(1, 0, 2))


def solution(mesh):
    spread_over = ("blk", "grp")
    in_specs = (
        P(None, spread_over),
        P(None, spread_over),
        P(None, spread_over),
        P(None, spread_over),
        P(spread_over),
        P(spread_over),
        P(None, spread_over),
        P(None, spread_over),
    )
    out_specs = (
        P(None, spread_over),
        P(None, spread_over),
        P(None, spread_over),
        P(None, spread_over),
        P(None, None, spread_over),
    )
    inner = functools.partial(body, mesh.shape["blk"], mesh.shape["grp"])
    return jax.shard_map(inner, mesh=mesh, in_specs=in_specs, out_specs=out_specs, check_vma=False)
```
